512 devices in a mesh: bucket: 16 (over x_hi, y), shard: 32 (over z, x_lo, core).
Axes of the slice: x: 4 (x_hi: 2, x_lo: 2; x = x_hi * 2 + x_lo), y: 8, z: 8, core: 2. Of those that a mesh axis runs over, the one named last changes fastest.
Arguments:
- source_slab: float32 [524288, 256], P(('bucket', 'shard')), may hold values from -1.5 to 1.5
- source_state: float32 [524288], P(('bucket', 'shard')), may hold values from 0.001 to 0.1
- dest_slab: float32 [524288, 256], P(('bucket', 'shard')), may hold values from -1.5 to 1.5
- dest_state: float32 [524288], P(('bucket', 'shard')), may hold values from 0.001 to 0.1
- source_rows: int32 [524288], P(('bucket', 'shard')), may hold values from 0 to 1023
- target_owner: int32 [524288, 1], P(('bucket', 'shard')), may hold values from 0 to 31; in each aligned block of 1024 rows (0 to 1023, 1024 to 2047, ...) at most 48 rows name the same one
- target_rows: int32 [524288], P(('bucket', 'shard')), may hold values from 0 to 1023
- negative_owner: int32 [1048576, 1], P(('bucket', 'shard')), may hold values from 0 to 31; in each aligned block of 2048 rows (0 to 2047, 2048 to 4095, ...) at most 96 rows name the same one
- negative_rows: int32 [1048576], P(('bucket', 'shard')), may hold values from 0 to 1023
- edge_count: int32 [512], P(('bucket', 'shard')), may hold values from 256 to 1024
- matching: int32 [16], replicated, may hold values from 0 to 15, as said below
Outputs:
- updated_source: float32 [524288, 256], P(('bucket', 'shard'))
- updated_source_state: float32 [524288], P(('bucket', 'shard'))
- incoming_dest: float32 [524288, 256], P(('bucket', 'shard'))
- incoming_dest_state: float32 [524288], P(('bucket', 'shard'))
The draws below stay inside these ranges and needn't reach their ends.
Inputs may be any that keep to these rules, and one draw needn't show every extreme that they name: `target_owner`: among the edges of one index pair, at most 48 name one owner. `negative_owner`: among the negatives of one index pair, at most 96 name one owner. matching[g] = g XOR m for one m from 1 to 15, the same for all g.
All inputs are finite; a program needn't handle non-finite values.
Results may differ from the reference program's by a relative error of at most 0.0023.
Values may be sent and summed in bfloat16 or wider, within the bound.
A program may use at most 64 MiB of HBM per device.

```python
import math
import jax
import jax.numpy as jnp
import numpy as np
from jax import lax

D = 256
ROWS_DEV = 1024
EDGES_DEV = 1024
NEG_DEV = 2048
CAP_EDGE = 48
CAP_NEG = 96
N_BUCKET = 16
N_SHARD = 32


def draw_edge_count(key, part):
    key = jax.random.fold_in(key, 11)
    devices_all = N_BUCKET * N_SHARD
    counts = jax.random.randint(jax.random.fold_in(key, 1), (devices_all,), EDGES_DEV // 4, EDGES_DEV + 1, dtype=jnp.int32)
    chosen = jax.random.randint(jax.random.fold_in(key, 2), (), 0, devices_all, dtype=jnp.int32)
    full_count = jnp.full((devices_all,), EDGES_DEV, dtype=jnp.int32)
    return jnp.where(jnp.arange(devices_all, dtype=jnp.int32) == chosen, full_count, counts)


def draw_matching(key, part):
    key = jax.random.fold_in(key, 12)
    partner_mask = jax.random.randint(key, (), 1, N_BUCKET, dtype=jnp.int32)
    return jnp.bitwise_xor(jnp.arange(N_BUCKET, dtype=jnp.int32), partner_mask)


def place_ends(drawn, rng, low, high):
    place = [jax.random.randint(jax.random.fold_in(rng, axis), (), 0, length) for axis, length in enumerate(drawn.shape)]
    main_axis = drawn.shape.index(max(drawn.shape))
    beside = place[:main_axis] + [(place[main_axis] + 1) % drawn.shape[main_axis]] + place[main_axis + 1:]
    return drawn.at[tuple(place)].set(low).at[tuple(beside)].set(high)


def shard_levels(rng, dims, cuts, low, largest):
    level = 1.0
    for axis_at, shards_of in cuts:
        heights = jax.random.uniform(jax.random.fold_in(jax.random.fold_in(rng, 6), axis_at), (shards_of,), jnp.float32, low / len(cuts), largest / len(cuts))
        level = level * jnp.repeat(jnp.exp(heights), dims[axis_at] // shards_of).reshape((-1,) + (1,) * (len(dims) - 1 - axis_at))
    return level


def assign_block(stream_key, own, number, rows, number_of, top, limit, slope):
    ranking = jax.random.permutation(stream_key, number_of)
    packed, usual = portions_of(number_of, rows * top, limit, slope, True), portions_of(number_of, rows * top, limit, slope, False)
    places = jnp.arange(number_of)

    def named(sizes, offset_by):
        used = int((sizes > 0).sum())
        fixed = max(1, used // 4)
        passed = fixed + (places - fixed + offset_by * (used - fixed)) % max(1, number_of - fixed)
        return jnp.zeros((number_of,), jnp.int32).at[ranking[jnp.where(places < fixed, places, passed)]].set(jnp.asarray(sizes, jnp.int32))

    sizes = jnp.where(number % 4 == 0, named(packed, number // 4), named(usual, number - number // 4 - 1))
    mixed = jax.random.permutation(jax.random.fold_in(own, 3), number_of)
    giver, taker = mixed[0:number_of // 2 * 2:2], mixed[1:number_of // 2 * 2:2]
    room = jnp.minimum(sizes[giver] - 1, limit - sizes[taker]) // 2
    room = jnp.where((giver == ranking[0]) | (taker == ranking[0]) | (sizes[taker] == 0), 0, jnp.maximum(room, 0))
    passed = jax.random.randint(jax.random.fold_in(own, 4), (number_of // 2,), 0, 1 << 20) % (room + 1)
    sizes = sizes.at[giver].add(-passed).at[taker].add(passed)
    items = jnp.searchsorted(jnp.cumsum(sizes), jnp.arange(rows * top), side="right").astype(jnp.int32)
    table = items.reshape(top, rows).T
    table = table[jax.random.permutation(jax.random.fold_in(own, 1), rows)]
    offset_by = jax.random.randint(jax.random.fold_in(own, 2), (rows, 1), 0, top)
    return jnp.take_along_axis(table, (jnp.arange(top)[None, :] + offset_by) % top, axis=1)


def portions_of(number_of, total, bound, skew, full):
    weights = [(1 << 20) // math.isqrt(grade ** skew) + 1 for grade in range(1, number_of + 1)]
    largest = bound if full else min(bound, max(-(-total // number_of), total * weights[0] // sum(weights)))
    least = 1 if total - largest >= number_of - 1 else 0
    given, surplus = [largest] + [least] * (number_of - 1), total - largest - least * (number_of - 1)
    while surplus > 0:
        movable = [i for i in range(1, number_of) if given[i] < largest] or [i for i in range(1, number_of) if given[i] < bound]
        mass, left = sum([weights[i] for i in movable]), surplus
        for i in movable:
            addition = min(bound - given[i], max(1, left * weights[i] // mass), surplus)
            given[i] = given[i] + addition
            surplus = surplus - addition
    return np.array(given)


def bell_draw(own_key, extent, scale, limit, split=(), held_as=jnp.bfloat16):
    drawn = scale * jax.random.normal(own_key, extent, jnp.float32)
    if split:
        drawn = drawn * shard_levels(own_key, extent, split, -0.22, 0.18)
    return jnp.clip(drawn, -limit, limit).astype(held_as)


def setup_inputs(seed: int = 0) -> dict:
    key_of = jax.random.split(jax.random.key(seed), 12)
    source_slab = bell_draw(key_of[0], (N_BUCKET * N_SHARD * ROWS_DEV, D), 0.25, 1.5, ((0, 512),), jnp.float32)
    source_state = jnp.clip(jnp.exp(math.log(0.1) - 4.6051702 * jax.random.uniform(key_of[1], (N_BUCKET * N_SHARD * ROWS_DEV,), jnp.float32) ** shard_levels(key_of[1], (N_BUCKET * N_SHARD * ROWS_DEV,), ((0, 512),), -0.2, 0.2)), 0.001, 0.1)
    dest_slab = bell_draw(key_of[2], (N_BUCKET * N_SHARD * ROWS_DEV, D), 0.25, 1.5, ((0, 512),), jnp.float32)
    dest_state = jnp.clip(jnp.exp(math.log(0.1) - 4.6051702 * jax.random.uniform(key_of[3], (N_BUCKET * N_SHARD * ROWS_DEV,), jnp.float32) ** shard_levels(key_of[3], (N_BUCKET * N_SHARD * ROWS_DEV,), ((0, 512),), -0.2, 0.2)), 0.001, 0.1)
    source_rows = place_ends(jax.random.randint(key_of[4], (N_BUCKET * N_SHARD * EDGES_DEV,), 0, ROWS_DEV), jax.random.fold_in(key_of[4], 1), 0, ROWS_DEV - 1).astype(jnp.int32)
    target_owner_keys = jax.random.split(jax.random.fold_in(key_of[5], 1), (N_BUCKET * N_SHARD * EDGES_DEV) // EDGES_DEV)
    target_owner_turns = jax.random.permutation(jax.random.fold_in(key_of[5], 3), (N_BUCKET * N_SHARD * EDGES_DEV) // EDGES_DEV)
    target_owner = jax.vmap(lambda own, number: assign_block(jax.random.fold_in(key_of[5], 2), own, number, EDGES_DEV, N_SHARD, 1, CAP_EDGE, 1))(target_owner_keys, target_owner_turns).reshape((N_BUCKET * N_SHARD * EDGES_DEV, 1))
    target_rows = place_ends(jax.random.randint(key_of[6], (N_BUCKET * N_SHARD * EDGES_DEV,), 0, ROWS_DEV), jax.random.fold_in(key_of[6], 1), 0, ROWS_DEV - 1).astype(jnp.int32)
    negative_owner_keys = jax.random.split(jax.random.fold_in(key_of[7], 1), (N_BUCKET * N_SHARD * NEG_DEV) // NEG_DEV)
    negative_owner_turns = jax.random.permutation(jax.random.fold_in(key_of[7], 3), (N_BUCKET * N_SHARD * NEG_DEV) // NEG_DEV)
    negative_owner = jax.vmap(lambda own, number: assign_block(jax.random.fold_in(key_of[7], 2), own, number, NEG_DEV, N_SHARD, 1, CAP_NEG, 1))(negative_owner_keys, negative_owner_turns).reshape((N_BUCKET * N_SHARD * NEG_DEV, 1))
    negative_rows = place_ends(jax.random.randint(key_of[8], (N_BUCKET * N_SHARD * NEG_DEV,), 0, ROWS_DEV), jax.random.fold_in(key_of[8], 1), 0, ROWS_DEV - 1).astype(jnp.int32)
    edge_count = draw_edge_count(jax.random.fold_in(key_of[11], 71), 0)
    matching = draw_matching(jax.random.fold_in(key_of[11], 71), 0)
    return dict(source_slab=source_slab, source_state=source_state, dest_slab=dest_slab, dest_state=dest_state, source_rows=source_rows, target_owner=target_owner, target_rows=target_rows, negative_owner=negative_owner, negative_rows=negative_rows, edge_count=edge_count, matching=matching)


learn_rate = 0.1
epsilon = 1e-06

def adagrad_rows(table_rows, row_state, row_grad):
    fresh_state = row_state + lax.optimization_barrier(jnp.mean(row_grad * row_grad, axis=1))
    return (table_rows - learn_rate * row_grad / (jnp.sqrt(fresh_state)[:, None] + epsilon), fresh_state)

def device_terms(table_rows, partition, rows_here, target_index, negative_index, count_limit):
    sources = lax.optimization_barrier(table_rows[rows_here].astype(jnp.bfloat16)).astype(jnp.float32)
    targets = partition[target_index]
    negatives = partition[negative_index]
    positive = lax.optimization_barrier(jnp.sum(sources * targets, axis=1))
    live_mask = (jnp.arange(rows_here.shape[0], dtype=jnp.int32) < count_limit).astype(jnp.float32)
    pos_coef = -live_mask * jax.nn.sigmoid(-positive)
    scores = jnp.dot(sources, negatives.T, precision=lax.Precision.HIGHEST)
    weights = live_mask[:, None] * NEG_DEV ** (-0.5) * jax.nn.sigmoid(scores)
    weights = lax.optimization_barrier(weights.astype(jnp.bfloat16)).astype(jnp.float32)
    source_grad = pos_coef[:, None] * targets + jnp.dot(weights, negatives, precision=lax.Precision.HIGHEST)
    negative_grad = jnp.dot(weights.T, sources, precision=lax.Precision.HIGHEST).astype(jnp.bfloat16)
    target_grad = (pos_coef[:, None] * sources).astype(jnp.bfloat16)
    summed = jnp.zeros(table_rows.shape, jnp.float32).at[rows_here].add(source_grad)
    return (summed, target_grad, negative_grad)

def reference(source_slab, source_state, dest_slab, dest_state, source_rows, target_owner, target_rows, negative_owner, negative_rows, edge_count, matching):
    source_all = source_slab.reshape(N_BUCKET, N_SHARD, ROWS_DEV, D)
    source_sums = source_state.reshape(N_BUCKET, N_SHARD, ROWS_DEV)
    dest_all = dest_slab.reshape(N_BUCKET, N_SHARD * ROWS_DEV, D)
    dest_sums = dest_state.reshape(N_BUCKET, N_SHARD * ROWS_DEV)
    rows_all = source_rows.reshape(N_BUCKET, N_SHARD, EDGES_DEV)
    target_all = (target_owner[:, 0] * ROWS_DEV + target_rows).astype(jnp.int32).reshape(N_BUCKET, N_SHARD, EDGES_DEV)
    negative_all = (negative_owner[:, 0] * ROWS_DEV + negative_rows).astype(jnp.int32).reshape(N_BUCKET, N_SHARD, NEG_DEV)
    count_all = edge_count.reshape(N_BUCKET, N_SHARD)
    source_out = []
    source_state_out = []
    dest_out = []
    dest_state_out = []
    for group_index in range(N_BUCKET):
        partition = lax.optimization_barrier(dest_all[group_index].astype(jnp.bfloat16)).astype(jnp.float32)

        def one_shard(dest_grad, pieces):
            table_rows, row_state, rows_here, target_index, negative_index, count_limit = pieces
            summed, target_grad, negative_grad = device_terms(table_rows, partition, rows_here, target_index, negative_index, count_limit)
            new_rows, new_state = adagrad_rows(table_rows, row_state, summed)
            dest_grad = dest_grad.at[target_index].add(target_grad.astype(jnp.float32))
            dest_grad = dest_grad.at[negative_index].add(negative_grad.astype(jnp.float32))
            return (dest_grad, (new_rows, new_state))
        dest_grad, outputs = lax.scan(one_shard, jnp.zeros((N_SHARD * ROWS_DEV, D), jnp.float32), (source_all[group_index], source_sums[group_index], rows_all[group_index], target_all[group_index], negative_all[group_index], count_all[group_index]))
        source_out.append(outputs[0])
        source_state_out.append(outputs[1])
        updated_rows, updated_state = adagrad_rows(dest_all[group_index], dest_sums[group_index], dest_grad)
        dest_out.append(updated_rows)
        dest_state_out.append(updated_state)
    updated_source = jnp.stack(source_out).reshape(N_BUCKET * N_SHARD * ROWS_DEV, D)
    updated_source_state = jnp.stack(source_state_out).reshape(N_BUCKET * N_SHARD * ROWS_DEV)
    incoming_dest = jnp.stack(dest_out)[matching].reshape(N_BUCKET * N_SHARD * ROWS_DEV, D)
    incoming_dest_state = jnp.stack(dest_state_out)[matching].reshape(N_BUCKET * N_SHARD * ROWS_DEV)
    return (updated_source, updated_source_state, incoming_dest, incoming_dest_state)
```

```python
import functools

import jax
import jax.numpy as jnp
from jax import lax
from jax.experimental import pallas as pl
from jax.experimental.pallas import tpu as pltpu
from jax.sharding import PartitionSpec as P

learn_rate = 0.1
epsilon = 1e-06
PLANE = 4
F32, BF16 = jnp.float32, jnp.bfloat16


def sigmoid(x):
    return 0.5 + 0.5 * jnp.tanh(0.5 * x)


def dot(a, b, ca=1, cb=0):
    return lax.dot_general(a, b, (((ca,), (cb,)), ((), ())), preferred_element_type=F32)


def iota(shape, dim):
    return lax.broadcasted_iota(jnp.int32, shape, dim).astype(F32)


def ones_where(mask):
    return jnp.where(mask, 1.0, 0.0).astype(BF16)


def offset_of(k, planes):
    i = k % planes
    size = i // 2 + 1
    dz = jnp.where(i == planes - 1, 0, size * (1 - 2 * (i % 2)))
    return dz, PLANE - 1 - k // planes


def partner(me, k, planes, sign):
    dz, dw = offset_of(k, planes)
    z = (me // PLANE + sign * dz + planes) % planes
    return z * PLANE + (me % PLANE + sign * dw + PLANE) % PLANE


def running_place(onehot):
    owners, n = onehot.shape
    width = 256
    upto = ones_where(iota((width, width), 0) <= iota((width, width), 1))
    carry = jnp.zeros((owners, 1), F32)
    parts = []
    for start in range(0, n, width):
        piece = onehot[:, start : start + width]
        count = dot(piece, upto) + carry
        carry = count[:, width - 1 : width]
        parts.append(jnp.sum(count * piece.astype(F32), axis=0, keepdims=True) - 1.0)
    return jnp.concatenate(parts, axis=1)


def step_kernel(
    shards,
    edge_slots,
    neg_weight,
    dest_ref,
    source_ref,
    src_rows_ref,
    edge_owner_ref,
    edge_rows_ref,
    neg_owner_ref,
    neg_rows_ref,
    live_ref,
    dest_grad_ref,
    source_sum_ref,
    table,
    src,
    src_t,
    src_hot,
    place,
    ask,
    asked,
    send_rows,
    got_rows,
    send_grads,
    got_grads,
    weights,
    chosen,
    coef_hi,
    coef_lo,
    grad_t,
    ask_send,
    ask_recv,
    row_send,
    row_recv,
    grad_send,
    grad_recv,
):
    bucket = lax.axis_index("bucket")
    me = lax.axis_index("shard")
    planes = shards // PLANE
    edges = src_rows_ref.shape[1]
    rows, features = dest_ref.shape
    slots = send_rows.shape[1]
    wide = ask.shape[2]
    mesh_id = pl.DeviceIdType.MESH

    barrier = pltpu.get_barrier_semaphore()

    def greet(k, carry):
        pl.semaphore_signal(
            barrier, inc=1, device_id=(bucket, partner(me, k, planes, 1)), device_id_type=mesh_id
        )
        return carry

    lax.fori_loop(0, shards - 1, greet, 0)

    edge_owner = edge_owner_ref[...].astype(F32)
    neg_owner = neg_owner_ref[...].astype(F32)
    negs = neg_owner.shape[1]
    edge_hot = ones_where(iota((shards, edges), 0) == edge_owner)
    neg_hot = ones_where(iota((shards, negs), 0) == neg_owner)
    edge_place = running_place(edge_hot)
    neg_place = running_place(neg_hot)
    place[...] = jnp.where(live_ref[...] > 0.0, edge_place, -1.0)

    def asked_ids(hot, rows_ref, slot_row):
        row = rows_ref[...]
        high = (row // 32).astype(F32).astype(BF16)
        low = (row % 32).astype(F32).astype(BF16)
        left = jnp.concatenate([hot * high, hot * low, hot], axis=0)
        at = ones_where(iota((wide, hot.shape[1]), 0) == slot_row)
        return dot(left, at, 1, 1)

    found = asked_ids(edge_hot, edge_rows_ref, edge_place) + asked_ids(
        neg_hot, neg_rows_ref, neg_place + float(edge_slots)
    )
    ids = found[:shards] * 32.0 + found[shards : 2 * shards] + found[2 * shards :] - 1.0
    for owner in range(shards):
        ask[owner] = ids[owner : owner + 1, :]
    asked[me] = ask[me]

    pl.semaphore_wait(barrier, shards - 1)

    def ask_copy(to, frm):
        return pltpu.make_async_remote_copy(
            src_ref=ask.at[to],
            dst_ref=asked.at[frm],
            send_sem=ask_send.at[to],
            recv_sem=ask_recv.at[frm],
            device_id=(bucket, to),
            device_id_type=mesh_id,
        )

    def row_copy(to, frm):
        return pltpu.make_async_remote_copy(
            src_ref=send_rows.at[to],
            dst_ref=got_rows.at[frm],
            send_sem=row_send.at[to],
            recv_sem=row_recv.at[frm],
            device_id=(bucket, to),
            device_id_type=mesh_id,
        )

    def grad_copy(to, frm):
        return pltpu.make_async_remote_copy(
            src_ref=send_grads.at[to],
            dst_ref=got_grads.at[frm],
            send_sem=grad_send.at[to],
            recv_sem=grad_recv.at[frm],
            device_id=(bucket, to),
            device_id_type=mesh_id,
        )

    def start_ask(k, carry):
        ask_copy(partner(me, k, planes, 1), me).start()
        return carry

    lax.fori_loop(0, shards - 1, start_ask, 0)

    table[...] = dest_ref[...].astype(BF16)
    src_hot[...] = ones_where(iota((rows, edges), 0) == src_rows_ref[...].astype(F32))
    source_t = source_ref[...].T.astype(BF16)
    picked_t = dot(source_t, src_hot[...])
    src_t[...] = picked_t.astype(BF16)
    src[...] = picked_t.T.astype(BF16)
    grad_t[...] = jnp.zeros_like(grad_t)

    def look_up(who):
        line = asked[who]
        column = jnp.sum(
            jnp.where(iota((slots, wide), 0) == iota((slots, wide), 1), line, 0.0),
            axis=1,
            keepdims=True,
        )
        hot = ones_where(column == iota((slots, rows), 1))
        return dot(hot, table[...]).astype(BF16)

    def serve(k, carry):
        who = partner(me, k, planes, -1)
        ask_copy(who, who).wait_recv()
        send_rows[who] = look_up(who)
        row_copy(who, me).start()
        return carry

    lax.fori_loop(0, shards - 1, serve, 0)
    got_rows[me] = look_up(me)

    def score(who):
        fetched = got_rows[who]
        targets = fetched[:edge_slots].astype(F32)
        scores = dot(fetched[edge_slots:], src_t[...])
        weight = (live_ref[...] * neg_weight * sigmoid(scores)).astype(BF16)
        weights[who] = weight
        slot_row = jnp.where(edge_owner_ref[...] == who, place[...], -1.0)
        pick = ones_where(iota((edge_slots, edges), 0) == slot_row)
        chosen[who] = pick
        mixed = dot(jnp.concatenate([pick, weight], axis=0), src[...])
        sources = mixed[:edge_slots]
        positive = jnp.sum(sources * targets, axis=1, keepdims=True)
        coef = -sigmoid(-positive)
        part = coef * targets
        high = part.astype(BF16)
        coef_hi[who] = high
        coef_lo[who] = (part - high.astype(F32)).astype(BF16)
        return jnp.concatenate([coef * sources, mixed[edge_slots:]], axis=0).astype(BF16)

    got_grads[me] = score(me)

    def answer(k, carry):
        who = partner(me, k, planes, -1)
        row_copy(who, who).wait_recv()
        send_grads[who] = score(who)
        grad_copy(who, me).start()
        return carry

    lax.fori_loop(0, shards - 1, answer, 0)

    def source_part(who, carry):
        left = jnp.concatenate([got_rows[who][edge_slots:], coef_hi[who], coef_lo[who]], axis=0)
        right = jnp.concatenate([weights[who], chosen[who], chosen[who]], axis=0)
        grad_t[...] += dot(left, right, 0, 0)
        return carry

    lax.fori_loop(0, shards, source_part, 0)
    source_grad = grad_t[...].T
    high = source_grad.astype(BF16)
    low = (source_grad - high.astype(F32)).astype(BF16)
    source_sum_ref[...] = dot(src_hot[...], high) + dot(src_hot[...], low)

    def collect(who):
        hot = ones_where(iota((rows, slots), 0) == asked[who][:, :slots])
        return dot(hot, got_grads[who])

    dest_grad_ref[...] = collect(me)

    def gather_grads(k, carry):
        who = partner(me, k, planes, -1)
        grad_copy(who, who).wait_recv()
        dest_grad_ref[...] += collect(who)
        return carry

    lax.fori_loop(0, shards - 1, gather_grads, 0)

    def finish(k, carry):
        to = partner(me, k, planes, 1)
        ask_copy(to, me).wait_send()
        row_copy(to, me).wait_send()
        grad_copy(to, me).wait_send()
        return carry

    lax.fori_loop(0, shards - 1, finish, 0)


def gradients(dest_slab, source_slab, source_rows, edge_owner, edge_rows, neg_owner, neg_rows, live):
    shards = lax.axis_size("shard")
    edges = source_rows.shape[0]
    negs = neg_rows.shape[0]
    rows, features = dest_slab.shape
    edge_slots = 3 * edges // (2 * shards)
    neg_slots = 3 * negs // (2 * shards)
    slots = edge_slots + neg_slots
    wide = -(-slots // 128) * 128
    vmem = pl.BlockSpec(memory_space=pltpu.VMEM)
    dma = pltpu.SemaphoreType.DMA
    return pl.pallas_call(
        functools.partial(step_kernel, shards, edge_slots, negs ** (-0.5)),
        out_shape=(
            jax.ShapeDtypeStruct((rows, features), F32),
            jax.ShapeDtypeStruct((rows, features), F32),
        ),
        in_specs=[vmem] * 8,
        out_specs=(vmem, vmem),
        scratch_shapes=[
            pltpu.VMEM((rows, features), BF16),
            pltpu.VMEM((edges, features), BF16),
            pltpu.VMEM((features, edges), BF16),
            pltpu.VMEM((rows, edges), BF16),
            pltpu.VMEM((1, edges), F32),
            pltpu.VMEM((shards, 1, wide), F32),
            pltpu.VMEM((shards, 1, wide), F32),
            pltpu.VMEM((shards, slots, features), BF16),
            pltpu.VMEM((shards, slots, features), BF16),
            pltpu.VMEM((shards, slots, features), BF16),
            pltpu.VMEM((shards, slots, features), BF16),
            pltpu.VMEM((shards, neg_slots, edges), BF16),
            pltpu.VMEM((shards, edge_slots, edges), BF16),
            pltpu.VMEM((shards, edge_slots, features), BF16),
            pltpu.VMEM((shards, edge_slots, features), BF16),
            pltpu.VMEM((features, edges), F32),
            dma((shards,)),
            dma((shards,)),
            dma((shards,)),
            dma((shards,)),
            dma((shards,)),
            dma((shards,)),
        ],
        compiler_params=pltpu.CompilerParams(
            collective_id=0, has_side_effects=True, vmem_limit_bytes=56 << 20
        ),
        name="edge_step",
    )(dest_slab, source_slab, source_rows[None], edge_owner[None], edge_rows[None], neg_owner[None], neg_rows[None], live[None])


def adagrad_rows(table_rows, row_state, row_grad):
    fresh_state = row_state + jnp.mean(row_grad * row_grad, axis=1)
    return (
        table_rows - learn_rate * row_grad / (jnp.sqrt(fresh_state)[:, None] + epsilon),
        fresh_state,
    )


def carry_over(table_rows, row_state, matching):
    size = lax.axis_size("bucket")
    largest = jnp.maximum(jnp.max(jnp.abs(table_rows), axis=1), 1e-30)
    coded = jnp.round(table_rows * (32767.0 / largest)[:, None]).astype(jnp.int16)
    beside = jnp.stack([largest, row_state])

    def exchange(mask):
        pairs = [(i, i ^ mask) for i in range(size)]
        return lambda a, b: (lax.ppermute(a, "bucket", pairs), lax.ppermute(b, "bucket", pairs))

    coded, beside = lax.switch(
        matching[0] - 1, [exchange(mask) for mask in range(1, size)], coded, beside
    )
    return coded.astype(F32) * (beside[0] * (1.0 / 32767.0))[:, None], beside[1]


def per_device(
    source_slab,
    source_state,
    dest_slab,
    dest_state,
    source_rows,
    target_owner,
    target_rows,
    negative_owner,
    negative_rows,
    edge_count,
    matching,
):
    edges = source_rows.shape[0]
    live = (jnp.arange(edges, dtype=jnp.int32) < edge_count[0]).astype(F32)
    dest_grad, source_sum = gradients(
        dest_slab,
        source_slab,
        source_rows,
        target_owner[:, 0],
        target_rows,
        negative_owner[:, 0],
        negative_rows,
        live,
    )
    new_dest, new_dest_state = adagrad_rows(dest_slab, dest_state, dest_grad)
    incoming_rows, incoming_state = carry_over(new_dest, new_dest_state, matching)
    new_source, new_source_state = adagrad_rows(source_slab, source_state, source_sum)
    return (new_source, new_source_state, incoming_rows, incoming_state)


def solution(mesh):
    both = ("bucket", "shard")
    in_specs = (
        P(both, None),
        P(both),
        P(both, None),
        P(both),
        P(both),
        P(both, None),
        P(both),
        P(both, None),
        P(both),
        P(both),
        P(),
    )
    out_specs = (P(both, None), P(both), P(both, None), P(both))
    return jax.shard_map(
        per_device, mesh=mesh, in_specs=in_specs, out_specs=out_specs, check_vma=False
    )
```

```python
import functools

import jax
import jax.numpy as jnp
from jax import lax
from jax.experimental import pallas as pl
from jax.experimental.pallas import tpu as pltpu
from jax.sharding import PartitionSpec as P

learn_rate = 0.1
epsilon = 1e-06
CODE = 32767.0
PLANE = 4
F32, BF16 = jnp.float32, jnp.bfloat16


def sigmoid(x):
    return 0.5 + 0.5 * jnp.tanh(0.5 * x)


def dot(a, b, ca=1, cb=0):
    return lax.dot_general(a, b, (((ca,), (cb,)), ((), ())), preferred_element_type=F32)


def iota(shape, dim):
    return lax.broadcasted_iota(jnp.int32, shape, dim).astype(F32)


def ones_where(mask):
    return jnp.where(mask, 1.0, 0.0).astype(BF16)


def around(i):
    return (i + 1) // 2 * (2 * (i % 2) - 1)


def partner(me, k, planes):
    z = (me // PLANE + around(k // PLANE) + planes) % planes
    return z * PLANE + (me % PLANE + k) % PLANE


def column(row):
    n = row.shape[1]
    return jnp.broadcast_to(row, (n, n)).T[:, :1]


def row_of(col):
    n = col.shape[0]
    return jnp.broadcast_to(col, (n, n)).T[:1, :]


def running_place(onehot):
    owners, n = onehot.shape
    width = 256
    upto = ones_where(iota((width, width), 0) <= iota((width, width), 1))
    carry = jnp.zeros((owners, 1), F32)
    parts = []
    for start in range(0, n, width):
        piece = onehot[:, start : start + width]
        count = dot(piece, upto) + carry
        carry = count[:, width - 1 : width]
        parts.append(jnp.sum(count * piece.astype(F32), axis=0, keepdims=True) - 1.0)
    return jnp.concatenate(parts, axis=1)


def step_kernel(
    edge_slots,
    neg_weight,
    dest_ref,
    dest_state_ref,
    source_ref,
    source_state_ref,
    src_rows_ref,
    edge_owner_ref,
    edge_rows_ref,
    neg_owner_ref,
    neg_rows_ref,
    live_ref,
    new_source_ref,
    new_source_state_ref,
    coded_ref,
    beside_ref,
    tables,
    src,
    src_t,
    src_hot,
    place,
    ask,
    asked,
    mate_ask,
    mate_asked,
    send_rows,
    got_rows,
    send_grads,
    got_grads,
    weights,
    chosen,
    coef_hi,
    coef_lo,
    grad_t,
    dest_grad,
    ask_send,
    ask_recv,
    mate_send,
    mate_recv,
    table_send,
    table_recv,
    row_send,
    row_recv,
    grad_send,
    grad_recv,
):
    bucket = lax.axis_index("bucket")
    me = lax.axis_index("shard")
    z, w = me // PLANE, me % PLANE
    planes = tables.shape[0]
    half = planes // 2
    shards = planes * PLANE
    edges = src_rows_ref.shape[1]
    rows, features = dest_ref.shape
    chunk = rows // 2
    slots = got_rows.shape[1]
    wide = ask.shape[2]

    def copy_to(to, src_ref, dst_ref, send_sem, recv_sem):
        return pltpu.make_async_remote_copy(
            src_ref=src_ref,
            dst_ref=dst_ref,
            send_sem=send_sem,
            recv_sem=recv_sem,
            device_id=(bucket, to),
            device_id_type=pl.DeviceIdType.MESH,
        )

    def ask_copy(to, frm):
        return copy_to(to, ask.at[to], asked.at[frm], ask_send.at[to], ask_recv.at[frm])

    def mate_copy(to, frm):
        return copy_to(
            z * PLANE + to, mate_ask.at[to], mate_asked.at[frm], mate_send.at[to], mate_recv.at[frm]
        )

    def table_copy(way, step, part):
        frm = (z - way * step + planes) % planes
        at = tables.at[frm, pl.ds(part * chunk, chunk)]
        return copy_to(
            (z + way + planes) % planes * PLANE + w,
            at,
            at,
            table_send.at[(way + 1) // 2, step, part],
            table_recv.at[frm, part],
        )

    def row_copy(to, frm, plane):
        return copy_to(
            z * PLANE + to,
            send_rows.at[plane, to],
            got_rows.at[plane * PLANE + frm],
            row_send.at[plane, to],
            row_recv.at[plane * PLANE + frm],
        )

    def grad_copy(to, frm):
        return copy_to(to, send_grads.at[to], got_grads.at[frm], grad_send.at[to], grad_recv.at[frm])

    barrier = pltpu.get_barrier_semaphore()

    def greet(k, carry):
        pl.semaphore_signal(
            barrier,
            inc=1,
            device_id=(bucket, partner(me, k, planes)),
            device_id_type=pl.DeviceIdType.MESH,
        )
        return carry

    lax.fori_loop(1, shards, greet, 0)
    tables[z] = dest_ref[...].astype(BF16)
    pl.semaphore_wait(barrier, shards - 1)

    def parts_of(way, step):
        return (0, 1) if step < half - 1 else ((0,) if way > 0 else (1,))

    def pass_on(step):
        for part in (0, 1):
            for way in (1, -1):
                if part in parts_of(way, step):
                    table_copy(way, step, part).start()

    pass_on(0)

    edge_owner = edge_owner_ref[...].astype(F32)
    neg_owner = neg_owner_ref[...].astype(F32)
    negs = neg_owner.shape[1]
    edge_hot = ones_where(iota((shards, edges), 0) == edge_owner)
    neg_hot = ones_where(iota((shards, negs), 0) == neg_owner)
    edge_place = running_place(edge_hot)
    neg_place = running_place(neg_hot)
    place[...] = jnp.where(live_ref[...] > 0.0, edge_place, -1.0)

    def asked_ids(hot, rows_ref, slot_row):
        row = rows_ref[...]
        high = (row // 32).astype(F32).astype(BF16)
        low = (row % 32).astype(F32).astype(BF16)
        left = jnp.concatenate([hot * high, hot * low, hot], axis=0)
        at = ones_where(iota((wide, hot.shape[1]), 0) == slot_row)
        return dot(left, at, 1, 1)

    found = asked_ids(edge_hot, edge_rows_ref, edge_place) + asked_ids(
        neg_hot, neg_rows_ref, neg_place + float(edge_slots)
    )
    ids = found[:shards] * 32.0 + found[shards : 2 * shards] + found[2 * shards :] - 1.0
    for owner in range(shards):
        line = ids[owner : owner + 1, :]
        ask[owner] = line
        mate_ask[owner % PLANE, owner // PLANE] = line
    asked[me] = ask[me]
    mate_asked[w] = mate_ask[w]
    for k in range(1, PLANE):
        mate_copy((w + k) % PLANE, w).start()

    def start_ask(k, carry):
        ask_copy(partner(me, k, planes), me).start()
        return carry

    lax.fori_loop(1, shards, start_ask, 0)

    src_hot[...] = ones_where(iota((rows, edges), 0) == src_rows_ref[...].astype(F32))
    source_t = source_ref[...].T.astype(BF16)
    picked_t = dot(source_t, src_hot[...])
    src_t[...] = picked_t.astype(BF16)
    src[...] = picked_t.T.astype(BF16)
    grad_t[...] = jnp.zeros_like(grad_t)
    for k in range(1, PLANE):
        mate_copy((w + k) % PLANE, (w + k) % PLANE).wait_recv()

    def serve(plane):
        hots = []
        for k in range(PLANE):
            line = mate_asked[(w + k) % PLANE, plane]
            spread = jnp.where(iota((slots, wide), 0) == iota((slots, wide), 1), line, 0.0)
            at = jnp.sum(spread, axis=1, keepdims=True)
            hots.append(ones_where(at == iota((slots, rows), 1)))
        found = dot(jnp.concatenate(hots, axis=0), tables[plane]).astype(BF16)
        for k in range(1, PLANE):
            to = (w + k) % PLANE
            send_rows[plane, to] = found[k * slots : (k + 1) * slots]
            row_copy(to, w, plane).start()
        got_rows[plane * PLANE + w] = found[:slots]

    def score(who):
        fetched = got_rows[who]
        targets = fetched[:edge_slots].astype(F32)
        scores = dot(fetched[edge_slots:], src_t[...])
        weight = (live_ref[...] * neg_weight * sigmoid(scores)).astype(BF16)
        weights[who] = weight
        slot_row = jnp.where(edge_owner_ref[...] == who, place[...], -1.0)
        pick = ones_where(iota((edge_slots, edges), 0) == slot_row)
        chosen[who] = pick
        mixed = dot(jnp.concatenate([pick, weight], axis=0), src[...])
        sources = mixed[:edge_slots]
        positive = jnp.sum(sources * targets, axis=1, keepdims=True)
        coef = -sigmoid(-positive)
        part = coef * targets
        high = part.astype(BF16)
        coef_hi[who] = high
        coef_lo[who] = (part - high.astype(F32)).astype(BF16)
        return jnp.concatenate([coef * sources, mixed[edge_slots:]], axis=0).astype(BF16)

    def answer(k, carry):
        who = partner(me, k, planes)
        mine = (w + k) % PLANE

        @pl.when(mine != w)
        def _():
            row_copy(w, mine, who // PLANE).wait_recv()

        send_grads[who] = score(who)
        grad_copy(who, me).start()
        return carry

    def serve_next(i, carry):
        serve((z + around(i) + planes) % planes)
        return carry

    def arrive(step):
        for part in (0, 1):
            for way in (1, -1):
                if part in parts_of(way, step - 1):
                    frm = (z - way * step + planes) % planes
                    at = tables.at[frm, pl.ds(part * chunk, chunk)]
                    copy_to(
                        (z - way + planes) % planes * PLANE + w,
                        at,
                        at,
                        table_send.at[0, 0, 0],
                        table_recv.at[frm, part],
                    ).wait_recv()
                    if step < half and part in parts_of(way, step):
                        table_copy(way, step, part).start()

    serve(z)
    for step in range(1, half + 1):
        arrive(step)
        lax.fori_loop(2 * step - 1, min(2 * step + 1, planes), serve_next, 0)
        if step == 1:
            got_grads[me] = score(me)
            lax.fori_loop(1, PLANE, answer, 0)
        else:
            lax.fori_loop((2 * step - 3) * PLANE, (2 * step - 1) * PLANE, answer, 0)
    lax.fori_loop((planes - 1) * PLANE, shards, answer, 0)

    def source_part(who, carry):
        left = jnp.concatenate([got_rows[who][edge_slots:], coef_hi[who], coef_lo[who]], axis=0)
        right = jnp.concatenate([weights[who], chosen[who], chosen[who]], axis=0)
        grad_t[...] += dot(left, right, 0, 0)
        return carry

    lax.fori_loop(0, shards, source_part, 0)
    source_grad = grad_t[...].T
    high = source_grad.astype(BF16)
    low = (source_grad - high.astype(F32)).astype(BF16)
    new_source_ref[...] = dot(src_hot[...], high) + dot(src_hot[...], low)
    block = 128

    def update(grad, table_ref, state_ref, at):
        mean = jnp.sum(grad * grad, axis=1, keepdims=True) * (1.0 / features)
        state = column(state_ref[:, at]) + mean
        return table_ref[at, :] - grad * (learn_rate / (jnp.sqrt(state) + epsilon)), state

    def update_source(i, carry):
        at = pl.ds(pl.multiple_of(i * block, block), block)
        fresh, state = update(new_source_ref[at, :], source_ref, source_state_ref, at)
        new_source_ref[at, :] = fresh
        new_source_state_ref[:, at] = row_of(state)
        return carry

    lax.fori_loop(0, rows // block, update_source, 0)

    def collect(who):
        hot = ones_where(iota((rows, slots), 0) == asked[who][:, :slots])
        return dot(hot, got_grads[who])

    dest_grad[...] = collect(me)

    def gather_grads(k, carry):
        who = partner(me, k, planes)
        ask_copy(who, who).wait_recv()
        grad_copy(who, who).wait_recv()
        dest_grad[...] += collect(who)
        return carry

    lax.fori_loop(1, shards, gather_grads, 0)

    def update_dest(i, carry):
        at = pl.ds(pl.multiple_of(i * block, block), block)
        fresh, state = update(dest_grad[at, :], dest_ref, dest_state_ref, at)
        largest = jnp.maximum(jnp.max(jnp.abs(fresh), axis=1, keepdims=True), 1e-30)
        coded_ref[at, :] = jnp.round(fresh * (CODE / largest)).astype(jnp.int16)
        beside_ref[0:1, at] = row_of(largest)
        beside_ref[1:2, at] = row_of(state)
        return carry

    lax.fori_loop(0, rows // block, update_dest, 0)

    def sent(k, carry):
        to = partner(me, k, planes)
        ask_copy(to, me).wait_send()
        grad_copy(to, me).wait_send()
        return carry

    lax.fori_loop(1, shards, sent, 0)
    for k in range(1, PLANE):
        to = (w + k) % PLANE
        mate_copy(to, w).wait_send()

        def rows_sent(plane, carry):
            row_copy(to, w, plane).wait_send()
            return carry

        lax.fori_loop(0, planes, rows_sent, 0)
    for step in range(half):
        for way in (1, -1):
            for part in parts_of(way, step):
                table_copy(way, step, part).wait_send()


def device_step(
    dest_slab,
    dest_state,
    source_slab,
    source_state,
    source_rows,
    edge_owner,
    edge_rows,
    neg_owner,
    neg_rows,
    live,
):
    shards = lax.axis_size("shard")
    planes = shards // PLANE
    edges = source_rows.shape[0]
    negs = neg_rows.shape[0]
    rows, features = dest_slab.shape
    edge_slots = 3 * edges // (2 * shards)
    neg_slots = 3 * negs // (2 * shards)
    slots = edge_slots + neg_slots
    wide = -(-slots // 128) * 128
    vmem = pl.BlockSpec(memory_space=pltpu.VMEM)
    dma = pltpu.SemaphoreType.DMA
    return pl.pallas_call(
        functools.partial(step_kernel, edge_slots, negs ** (-0.5)),
        out_shape=(
            jax.ShapeDtypeStruct((rows, features), F32),
            jax.ShapeDtypeStruct((1, rows), F32),
            jax.ShapeDtypeStruct((rows, features), jnp.int16),
            jax.ShapeDtypeStruct((2, rows), F32),
        ),
        in_specs=[vmem] * 10,
        out_specs=(vmem,) * 4,
        scratch_shapes=[
            pltpu.VMEM((planes, rows, features), BF16),
            pltpu.VMEM((edges, features), BF16),
            pltpu.VMEM((features, edges), BF16),
            pltpu.VMEM((rows, edges), BF16),
            pltpu.VMEM((1, edges), F32),
            pltpu.VMEM((shards, 1, wide), F32),
            pltpu.VMEM((shards, 1, wide), F32),
            pltpu.VMEM((PLANE, planes, 1, wide), F32),
            pltpu.VMEM((PLANE, planes, 1, wide), F32),
            pltpu.VMEM((planes, PLANE, slots, features), BF16),
            pltpu.VMEM((shards, slots, features), BF16),
            pltpu.VMEM((shards, slots, features), BF16),
            pltpu.VMEM((shards, slots, features), BF16),
            pltpu.VMEM((shards, neg_slots, edges), BF16),
            pltpu.VMEM((shards, edge_slots, edges), BF16),
            pltpu.VMEM((shards, edge_slots, features), BF16),
            pltpu.VMEM((shards, edge_slots, features), BF16),
            pltpu.VMEM((features, edges), F32),
            pltpu.VMEM((rows, features), F32),
            dma((shards,)),
            dma((shards,)),
            dma((PLANE,)),
            dma((PLANE,)),
            dma((2, planes // 2, 2)),
            dma((planes, 2)),
            dma((planes, PLANE)),
            dma((shards,)),
            dma((shards,)),
            dma((shards,)),
        ],
        compiler_params=pltpu.CompilerParams(
            collective_id=0, has_side_effects=True, vmem_limit_bytes=58 << 20
        ),
        name="edge_step",
    )(
        dest_slab,
        dest_state[None],
        source_slab,
        source_state[None],
        source_rows[None],
        edge_owner[None],
        edge_rows[None],
        neg_owner[None],
        neg_rows[None],
        live[None],
    )


def carry_over(coded, beside, matching):
    size = lax.axis_size("bucket")

    def exchange(mask):
        pairs = [(i, i ^ mask) for i in range(size)]
        return lambda a, b: (lax.ppermute(a, "bucket", pairs), lax.ppermute(b, "bucket", pairs))

    coded, beside = lax.switch(
        matching[0] - 1, [exchange(mask) for mask in range(1, size)], coded, beside
    )
    return coded.astype(F32) * (beside[0] * (1.0 / CODE))[:, None], beside[1]


def per_device(
    source_slab,
    source_state,
    dest_slab,
    dest_state,
    source_rows,
    target_owner,
    target_rows,
    negative_owner,
    negative_rows,
    edge_count,
    matching,
):
    edges = source_rows.shape[0]
    live = (jnp.arange(edges, dtype=jnp.int32) < edge_count[0]).astype(F32)
    new_source, new_source_state, coded, beside = device_step(
        dest_slab,
        dest_state,
        source_slab,
        source_state,
        source_rows,
        target_owner[:, 0],
        target_rows,
        negative_owner[:, 0],
        negative_rows,
        live,
    )
    incoming_rows, incoming_state = carry_over(coded, beside, matching)
    return (new_source, new_source_state[0], incoming_rows, incoming_state)


def solution(mesh):
    both = ("bucket", "shard")
    in_specs = (
        P(both, None),
        P(both),
        P(both, None),
        P(both),
        P(both),
        P(both, None),
        P(both),
        P(both, None),
        P(both),
        P(both),
        P(),
    )
    out_specs = (P(both, None), P(both), P(both, None), P(both))
    return jax.shard_map(
        per_device, mesh=mesh, in_specs=in_specs, out_specs=out_specs, check_vma=False
    )
```

```python
import functools

import jax
import jax.numpy as jnp
from jax import lax
from jax.experimental import pallas as pl
from jax.experimental.pallas import tpu as pltpu
from jax.sharding import PartitionSpec as P

learn_rate = 0.1
epsilon = 1e-06
CODE = 32767.0
BLOCK = 128
PLANE = 4
F32, BF16 = jnp.float32, jnp.bfloat16


def sigmoid(x):
    return 0.5 + 0.5 * jnp.tanh(0.5 * x)


def dot(a, b, ca=1, cb=0):
    return lax.dot_general(a, b, (((ca,), (cb,)), ((), ())), preferred_element_type=F32)


def iota(shape, dim):
    return lax.broadcasted_iota(jnp.int32, shape, dim).astype(F32)


def ones_where(mask):
    return jnp.where(mask, 1.0, 0.0).astype(BF16)


def around(i):
    return (i + 1) // 2 * (2 * (i % 2) - 1)


def partner(me, k, planes):
    z = (me // PLANE + around(k // PLANE) + planes) % planes
    return z * PLANE + (me % PLANE + k) % PLANE


def column(row):
    n = row.shape[1]
    return jnp.broadcast_to(row, (n, n)).T[:, :1]


def row_of(col):
    n = col.shape[0]
    return jnp.broadcast_to(col, (n, n)).T[:1, :]


def running_place(onehot):
    owners, n = onehot.shape
    width = 256
    upto = ones_where(iota((width, width), 0) <= iota((width, width), 1))
    carry = jnp.zeros((owners, 1), F32)
    parts = []
    for start in range(0, n, width):
        piece = onehot[:, start : start + width]
        count = dot(piece, upto) + carry
        carry = count[:, width - 1 : width]
        parts.append(jnp.sum(count * piece.astype(F32), axis=0, keepdims=True) - 1.0)
    return jnp.concatenate(parts, axis=1)


def update(grad, table_ref, state_ref, at):
    mean = jnp.sum(grad * grad, axis=1, keepdims=True) * (1.0 / grad.shape[1])
    state = column(state_ref[:, at]) + mean
    return table_ref[at, :] - grad * (learn_rate / (jnp.sqrt(state) + epsilon)), state


def step_kernel(
    edge_slots,
    neg_weight,
    dest_ref,
    source_ref,
    source_state_ref,
    src_rows_ref,
    edge_owner_ref,
    edge_rows_ref,
    neg_owner_ref,
    neg_rows_ref,
    live_ref,
    new_source_ref,
    new_source_state_ref,
    dest_grad,
    tables,
    src,
    src_t,
    src_hot,
    place,
    ask,
    asked,
    mate_ask,
    mate_asked,
    send_rows,
    got_rows,
    send_grads,
    got_grads,
    weights,
    chosen,
    coef_hi,
    coef_lo,
    grad_t,
    ask_send,
    ask_recv,
    mate_send,
    mate_recv,
    table_send,
    table_recv,
    row_send,
    row_recv,
    grad_send,
    grad_recv,
):
    bucket = lax.axis_index("bucket")
    me = lax.axis_index("shard")
    z, w = me // PLANE, me % PLANE
    planes = tables.shape[0]
    half = planes // 2
    shards = planes * PLANE
    edges = src_rows_ref.shape[1]
    rows, features = dest_ref.shape
    chunk = rows // 2
    slots = got_rows.shape[1]
    wide = ask.shape[2]

    def copy_to(to, src_ref, dst_ref, send_sem, recv_sem):
        return pltpu.make_async_remote_copy(
            src_ref=src_ref,
            dst_ref=dst_ref,
            send_sem=send_sem,
            recv_sem=recv_sem,
            device_id=(bucket, to),
            device_id_type=pl.DeviceIdType.MESH,
        )

    def ask_copy(to, frm):
        return copy_to(to, ask.at[to], asked.at[frm], ask_send.at[to], ask_recv.at[frm])

    def mate_copy(to, frm):
        return copy_to(
            z * PLANE + to, mate_ask.at[to], mate_asked.at[frm], mate_send.at[to], mate_recv.at[frm]
        )

    def table_copy(way, step, part):
        frm = (z - way * step + planes) % planes
        at = tables.at[frm, pl.ds(part * chunk, chunk)]
        return copy_to(
            (z + way + planes) % planes * PLANE + w,
            at,
            at,
            table_send.at[(way + 1) // 2, step, part],
            table_recv.at[frm, part],
        )

    def row_copy(to, frm, plane):
        return copy_to(
            z * PLANE + to,
            send_rows.at[plane, to],
            got_rows.at[plane * PLANE + frm],
            row_send.at[plane, to],
            row_recv.at[plane * PLANE + frm],
        )

    def grad_copy(to, frm):
        return copy_to(to, send_grads.at[to], got_grads.at[frm], grad_send.at[to], grad_recv.at[frm])

    barrier = pltpu.get_barrier_semaphore()

    def greet(k, carry):
        pl.semaphore_signal(
            barrier,
            inc=1,
            device_id=(bucket, partner(me, k, planes)),
            device_id_type=pl.DeviceIdType.MESH,
        )
        return carry

    lax.fori_loop(1, shards, greet, 0)
    tables[z] = dest_ref[...].astype(BF16)
    pl.semaphore_wait(barrier, shards - 1)

    def parts_of(way, step):
        return (0, 1) if step < half - 1 else ((0,) if way > 0 else (1,))

    def pass_on(step):
        for part in (0, 1):
            for way in (1, -1):
                if part in parts_of(way, step):
                    table_copy(way, step, part).start()

    pass_on(0)

    edge_owner = edge_owner_ref[...].astype(F32)
    neg_owner = neg_owner_ref[...].astype(F32)
    negs = neg_owner.shape[1]
    edge_hot = ones_where(iota((shards, edges), 0) == edge_owner)
    neg_hot = ones_where(iota((shards, negs), 0) == neg_owner)
    edge_place = running_place(edge_hot)
    neg_place = running_place(neg_hot)
    place[...] = jnp.where(live_ref[...] > 0.0, edge_place, -1.0)

    def asked_ids(hot, rows_ref, slot_row):
        row = rows_ref[...]
        high = (row // 32).astype(F32).astype(BF16)
        low = (row % 32).astype(F32).astype(BF16)
        left = jnp.concatenate([hot * high, hot * low, hot], axis=0)
        at = ones_where(iota((wide, hot.shape[1]), 0) == slot_row)
        return dot(left, at, 1, 1)

    found = asked_ids(edge_hot, edge_rows_ref, edge_place) + asked_ids(
        neg_hot, neg_rows_ref, neg_place + float(edge_slots)
    )
    ids = found[:shards] * 32.0 + found[shards : 2 * shards] + found[2 * shards :] - 1.0
    for owner in range(shards):
        line = ids[owner : owner + 1, :]
        ask[owner] = line
        mate_ask[owner % PLANE, owner // PLANE] = line
    asked[me] = ask[me]
    mate_asked[w] = mate_ask[w]
    for k in range(1, PLANE):
        mate_copy((w + k) % PLANE, w).start()

    def start_ask(k, carry):
        ask_copy(partner(me, k, planes), me).start()
        return carry

    lax.fori_loop(1, shards, start_ask, 0)

    src_hot[...] = ones_where(iota((rows, edges), 0) == src_rows_ref[...].astype(F32))
    source_t = source_ref[...].T.astype(BF16)
    picked_t = dot(source_t, src_hot[...])
    src_t[...] = picked_t.astype(BF16)
    src[...] = picked_t.T.astype(BF16)
    grad_t[...] = jnp.zeros_like(grad_t)
    for k in range(1, PLANE):
        mate_copy((w + k) % PLANE, (w + k) % PLANE).wait_recv()

    def serve(plane):
        hots = []
        for k in range(PLANE):
            line = mate_asked[(w + k) % PLANE, plane]
            spread = jnp.where(iota((slots, wide), 0) == iota((slots, wide), 1), line, 0.0)
            at = jnp.sum(spread, axis=1, keepdims=True)
            hots.append(ones_where(at == iota((slots, rows), 1)))
        found = dot(jnp.concatenate(hots, axis=0), tables[plane]).astype(BF16)
        for k in range(1, PLANE):
            to = (w + k) % PLANE
            send_rows[plane, to] = found[k * slots : (k + 1) * slots]
            row_copy(to, w, plane).start()
        got_rows[plane * PLANE + w] = found[:slots]

    def score(who):
        fetched = got_rows[who]
        targets = fetched[:edge_slots].astype(F32)
        scores = dot(fetched[edge_slots:], src_t[...])
        weight = (live_ref[...] * neg_weight * sigmoid(scores)).astype(BF16)
        weights[who] = weight
        slot_row = jnp.where(edge_owner_ref[...] == who, place[...], -1.0)
        pick = ones_where(iota((edge_slots, edges), 0) == slot_row)
        chosen[who] = pick
        mixed = dot(jnp.concatenate([pick, weight], axis=0), src[...])
        sources = mixed[:edge_slots]
        positive = jnp.sum(sources * targets, axis=1, keepdims=True)
        coef = -sigmoid(-positive)
        part = coef * targets
        high = part.astype(BF16)
        coef_hi[who] = high
        coef_lo[who] = (part - high.astype(F32)).astype(BF16)
        return jnp.concatenate([coef * sources, mixed[edge_slots:]], axis=0).astype(BF16)

    def answer(k, carry):
        who = partner(me, k, planes)
        mine = (w + k) % PLANE

        @pl.when(mine != w)
        def _():
            row_copy(w, mine, who // PLANE).wait_recv()

        send_grads[who] = score(who)
        grad_copy(who, me).start()
        return carry

    def serve_next(i, carry):
        serve((z + around(i) + planes) % planes)
        return carry

    def arrive(step):
        for part in (0, 1):
            for way in (1, -1):
                if part in parts_of(way, step - 1):
                    frm = (z - way * step + planes) % planes
                    at = tables.at[frm, pl.ds(part * chunk, chunk)]
                    copy_to(
                        (z - way + planes) % planes * PLANE + w,
                        at,
                        at,
                        table_send.at[0, 0, 0],
                        table_recv.at[frm, part],
                    ).wait_recv()
                    if step < half and part in parts_of(way, step):
                        table_copy(way, step, part).start()

    serve(z)
    for step in range(1, half + 1):
        arrive(step)
        lax.fori_loop(2 * step - 1, min(2 * step + 1, planes), serve_next, 0)
        if step == 1:
            got_grads[me] = score(me)
            lax.fori_loop(1, PLANE, answer, 0)
        else:
            lax.fori_loop((2 * step - 3) * PLANE, (2 * step - 1) * PLANE, answer, 0)
    lax.fori_loop((planes - 1) * PLANE, shards, answer, 0)

    def source_part(who, carry):
        left = jnp.concatenate([got_rows[who][edge_slots:], coef_hi[who], coef_lo[who]], axis=0)
        right = jnp.concatenate([weights[who], chosen[who], chosen[who]], axis=0)
        grad_t[...] += dot(left, right, 0, 0)
        return carry

    lax.fori_loop(0, shards, source_part, 0)
    source_grad = grad_t[...].T
    high = source_grad.astype(BF16)
    low = (source_grad - high.astype(F32)).astype(BF16)
    new_source_ref[...] = dot(src_hot[...], high) + dot(src_hot[...], low)

    def update_source(i, carry):
        at = pl.ds(pl.multiple_of(i * BLOCK, BLOCK), BLOCK)
        fresh, state = update(new_source_ref[at, :], source_ref, source_state_ref, at)
        new_source_ref[at, :] = fresh
        new_source_state_ref[:, at] = row_of(state)
        return carry

    lax.fori_loop(0, rows // BLOCK, update_source, 0)

    def collect(who):
        hot = ones_where(iota((rows, slots), 0) == asked[who][:, :slots])
        return dot(hot, got_grads[who])

    dest_grad[...] = collect(me)

    def gather_grads(k, carry):
        who = partner(me, k, planes)
        ask_copy(who, who).wait_recv()
        grad_copy(who, who).wait_recv()
        dest_grad[...] += collect(who)
        return carry

    lax.fori_loop(1, shards, gather_grads, 0)

    def sent(k, carry):
        to = partner(me, k, planes)
        ask_copy(to, me).wait_send()
        grad_copy(to, me).wait_send()
        return carry

    lax.fori_loop(1, shards, sent, 0)
    for k in range(1, PLANE):
        to = (w + k) % PLANE
        mate_copy(to, w).wait_send()

        def rows_sent(plane, carry):
            row_copy(to, w, plane).wait_send()
            return carry

        lax.fori_loop(0, planes, rows_sent, 0)
    for step in range(half):
        for way in (1, -1):
            for part in parts_of(way, step):
                table_copy(way, step, part).wait_send()


def device_step(
    dest_slab,
    source_slab,
    source_state,
    source_rows,
    edge_owner,
    edge_rows,
    neg_owner,
    neg_rows,
    live,
):
    shards = lax.axis_size("shard")
    planes = shards // PLANE
    edges = source_rows.shape[0]
    negs = neg_rows.shape[0]
    rows, features = dest_slab.shape
    edge_slots = 3 * edges // (2 * shards)
    neg_slots = 3 * negs // (2 * shards)
    slots = edge_slots + neg_slots
    wide = -(-slots // 128) * 128
    vmem = pl.BlockSpec(memory_space=pltpu.VMEM)
    dma = pltpu.SemaphoreType.DMA
    return pl.pallas_call(
        functools.partial(step_kernel, edge_slots, negs ** (-0.5)),
        out_shape=(
            jax.ShapeDtypeStruct((rows, features), F32),
            jax.ShapeDtypeStruct((1, rows), F32),
            jax.ShapeDtypeStruct((rows, features), F32),
        ),
        in_specs=[vmem] * 9,
        out_specs=(vmem,) * 3,
        scratch_shapes=[
            pltpu.VMEM((planes, rows, features), BF16),
            pltpu.VMEM((edges, features), BF16),
            pltpu.VMEM((features, edges), BF16),
            pltpu.VMEM((rows, edges), BF16),
            pltpu.VMEM((1, edges), F32),
            pltpu.VMEM((shards, 1, wide), F32),
            pltpu.VMEM((shards, 1, wide), F32),
            pltpu.VMEM((PLANE, planes, 1, wide), F32),
            pltpu.VMEM((PLANE, planes, 1, wide), F32),
            pltpu.VMEM((planes, PLANE, slots, features), BF16),
            pltpu.VMEM((shards, slots, features), BF16),
            pltpu.VMEM((shards, slots, features), BF16),
            pltpu.VMEM((shards, slots, features), BF16),
            pltpu.VMEM((shards, neg_slots, edges), BF16),
            pltpu.VMEM((shards, edge_slots, edges), BF16),
            pltpu.VMEM((shards, edge_slots, features), BF16),
            pltpu.VMEM((shards, edge_slots, features), BF16),
            pltpu.VMEM((features, edges), F32),
            dma((shards,)),
            dma((shards,)),
            dma((PLANE,)),
            dma((PLANE,)),
            dma((2, planes // 2, 2)),
            dma((planes, 2)),
            dma((planes, PLANE)),
            dma((shards,)),
            dma((shards,)),
            dma((shards,)),
        ],
        compiler_params=pltpu.CompilerParams(
            collective_id=0, has_side_effects=True, vmem_limit_bytes=58 << 20
        ),
        name="edge_step",
    )(
        dest_slab,
        source_slab,
        source_state[None],
        source_rows[None],
        edge_owner[None],
        edge_rows[None],
        neg_owner[None],
        neg_rows[None],
        live[None],
    )


def hand_over_kernel(
    mask,
    grad_ref,
    dest_ref,
    state_ref,
    rows_ref,
    new_state_ref,
    coded,
    beside,
    got,
    got_beside,
    send,
    recv,
    beside_send,
    beside_recv,
):
    bucket = lax.axis_index("bucket")
    to = bucket
    for bit in range(mask.bit_length()):
        if mask >> bit & 1:
            to = to + (1 - 2 * (bucket // (1 << bit) % 2)) * (1 << bit)
    to = (to, lax.axis_index("shard"))
    parts = beside.shape[0]
    size = dest_ref.shape[0] // parts

    def copies(part):
        at = pl.ds(part * size, size)
        pairs = (
            (coded.at[at], got.at[at], send, recv),
            (beside.at[part], got_beside.at[part], beside_send, beside_recv),
        )
        return [
            pltpu.make_async_remote_copy(
                src_ref=src_ref,
                dst_ref=dst_ref,
                send_sem=sent.at[part],
                recv_sem=came.at[part],
                device_id=to,
                device_id_type=pl.DeviceIdType.MESH,
            )
            for src_ref, dst_ref, sent, came in pairs
        ]

    barrier = pltpu.get_barrier_semaphore()
    pl.semaphore_signal(barrier, inc=1, device_id=to, device_id_type=pl.DeviceIdType.MESH)
    for part in range(parts):
        for start in range(0, size, BLOCK):
            at = pl.ds(part * size + start, BLOCK)
            fresh, state = update(grad_ref[at, :], dest_ref, state_ref, at)
            largest = jnp.maximum(jnp.max(jnp.abs(fresh), axis=1, keepdims=True), 1e-30)
            coded[at, :] = jnp.round(fresh * (CODE / largest)).astype(jnp.int16)
            beside[part, 0:1, start : start + BLOCK] = row_of(largest)
            beside[part, 1:2, start : start + BLOCK] = row_of(state)
        if part == 0:
            pl.semaphore_wait(barrier, 1)
        for copy in copies(part):
            copy.start()
    for part in range(parts):
        for copy in copies(part):
            copy.wait_recv()
        for start in range(0, size, BLOCK):
            at = pl.ds(part * size + start, BLOCK)
            scale = column(got_beside[part, 0:1, start : start + BLOCK]) * (1.0 / CODE)
            rows_ref[at, :] = got[at, :].astype(F32) * scale
            new_state_ref[:, at] = got_beside[part, 1:2, start : start + BLOCK]
    for part in range(parts):
        for copy in copies(part):
            copy.wait_send()


def hand_over(mask, dest_grad, dest_slab, dest_state):
    rows, features = dest_slab.shape
    parts = max(1, min(4, rows // BLOCK))
    vmem = pl.BlockSpec(memory_space=pltpu.VMEM)
    dma = pltpu.SemaphoreType.DMA
    return pl.pallas_call(
        functools.partial(hand_over_kernel, mask),
        out_shape=(
            jax.ShapeDtypeStruct((rows, features), F32),
            jax.ShapeDtypeStruct((1, rows), F32),
        ),
        in_specs=[vmem] * 3,
        out_specs=(vmem, vmem),
        scratch_shapes=[
            pltpu.VMEM((rows, features), jnp.int16),
            pltpu.VMEM((parts, 2, rows // parts), F32),
            pltpu.VMEM((rows, features), jnp.int16),
            pltpu.VMEM((parts, 2, rows // parts), F32),
            dma((parts,)),
            dma((parts,)),
            dma((parts,)),
            dma((parts,)),
        ],
        compiler_params=pltpu.CompilerParams(
            collective_id=mask, has_side_effects=True, vmem_limit_bytes=32 << 20
        ),
        name="hand_over",
    )(dest_grad, dest_slab, dest_state)


def per_device(
    source_slab,
    source_state,
    dest_slab,
    dest_state,
    source_rows,
    target_owner,
    target_rows,
    negative_owner,
    negative_rows,
    edge_count,
    matching,
):
    edges = source_rows.shape[0]
    live = (jnp.arange(edges, dtype=jnp.int32) < edge_count[0]).astype(F32)
    new_source, new_source_state, dest_grad = device_step(
        dest_slab,
        source_slab,
        source_state,
        source_rows,
        target_owner[:, 0],
        target_rows,
        negative_owner[:, 0],
        negative_rows,
        live,
    )
    incoming_rows, incoming_state = lax.switch(
        matching[0] - 1,
        [functools.partial(hand_over, mask) for mask in range(1, lax.axis_size("bucket"))],
        dest_grad,
        dest_slab,
        dest_state[None],
    )
    return (new_source, new_source_state[0], incoming_rows, incoming_state[0])


def solution(mesh):
    both = ("bucket", "shard")
    in_specs = (
        P(both, None),
        P(both),
        P(both, None),
        P(both),
        P(both),
        P(both, None),
        P(both),
        P(both, None),
        P(both),
        P(both),
        P(),
    )
    out_specs = (P(both, None), P(both), P(both, None), P(both))
    return jax.shard_map(
        per_device, mesh=mesh, in_specs=in_specs, out_specs=out_specs, check_vma=False
    )
```

```python
import functools

import jax
import jax.numpy as jnp
from jax import lax
from jax.experimental import pallas as pl
from jax.experimental.pallas import tpu as pltpu
from jax.sharding import PartitionSpec as P

learn_rate = 0.1
epsilon = 1e-06
CODE = 32767.0
BLOCK = 128
PLANE = 4
F32, BF16 = jnp.float32, jnp.bfloat16


def sigmoid(x):
    return 0.5 + 0.5 * jnp.tanh(0.5 * x)


def dot(a, b, ca=1, cb=0):
    return lax.dot_general(a, b, (((ca,), (cb,)), ((), ())), preferred_element_type=F32)


def iota(shape, dim):
    return lax.broadcasted_iota(jnp.int32, shape, dim).astype(F32)


def ones_where(mask):
    return jnp.where(mask, 1.0, 0.0).astype(BF16)


def around(i):
    return (i + 1) // 2 * (2 * (i % 2) - 1)


def partner(me, k, planes):
    z = (me // PLANE + around(k // PLANE) + planes) % planes
    return z * PLANE + (me % PLANE + k) % PLANE


def column(row):
    n = row.shape[1]
    return jnp.broadcast_to(row, (n, n)).T[:, :1]


def row_of(col):
    n = col.shape[0]
    return jnp.broadcast_to(col, (n, n)).T[:1, :]


def running_place(onehot):
    owners, n = onehot.shape
    width = 256
    upto = ones_where(iota((width, width), 0) <= iota((width, width), 1))
    carry = jnp.zeros((owners, 1), F32)
    parts = []
    for start in range(0, n, width):
        piece = onehot[:, start : start + width]
        count = dot(piece, upto) + carry
        carry = count[:, width - 1 : width]
        parts.append(jnp.sum(count * piece.astype(F32), axis=0, keepdims=True) - 1.0)
    return jnp.concatenate(parts, axis=1)


def update(grad, table_ref, state_ref, at):
    mean = jnp.sum(grad * grad, axis=1, keepdims=True) * (1.0 / grad.shape[1])
    state = column(state_ref[:, at]) + mean
    return table_ref[at, :] - grad * (learn_rate / (jnp.sqrt(state) + epsilon)), state


def step_kernel(
    edge_slots,
    neg_weight,
    dest_ref,
    source_ref,
    source_state_ref,
    src_rows_ref,
    edge_owner_ref,
    edge_rows_ref,
    neg_owner_ref,
    neg_rows_ref,
    count_ref,
    new_source_ref,
    new_source_state_ref,
    dest_grad,
    tables,
    src,
    src_t,
    src_hot,
    place,
    live_weight,
    ask,
    asked,
    mate_ask,
    mate_asked,
    send_rows,
    got_rows,
    send_grads,
    got_grads,
    weights,
    chosen,
    coef_hi,
    coef_lo,
    grad_t,
    side_grad,
    side_sum,
    side_scale,
    got_sum,
    got_scale,
    ask_send,
    ask_recv,
    mate_send,
    mate_recv,
    table_send,
    table_recv,
    row_send,
    row_recv,
    grad_send,
    grad_recv,
    sum_send,
    sum_recv,
    scale_send,
    scale_recv,
):
    bucket = lax.axis_index("bucket")
    me = lax.axis_index("shard")
    z, w = me // PLANE, me % PLANE
    planes = tables.shape[0]
    half = planes // 2
    shards = planes * PLANE
    edges = src_rows_ref.shape[1]
    rows, features = dest_ref.shape
    chunk = rows // 2
    slots = got_rows.shape[1]
    wide = ask.shape[2]

    def copy_to(to, src_ref, dst_ref, send_sem, recv_sem):
        return pltpu.make_async_remote_copy(
            src_ref=src_ref,
            dst_ref=dst_ref,
            send_sem=send_sem,
            recv_sem=recv_sem,
            device_id=(bucket, to),
            device_id_type=pl.DeviceIdType.MESH,
        )

    def route(k):
        off = around(k // PLANE)
        far = jnp.where(w < PLANE // 2, 1, -1)
        side = jnp.where(off == 0, 0, jnp.where(off < 0, 1, jnp.where(off == half, far, -1)))
        slot = jnp.where(off < 0, -off, off) + jnp.where(side < 0, half, 0)
        plane = (z + off + side + planes) % planes
        return plane * PLANE + (w + k) % PLANE, slot

    def ask_copy(k):
        who = partner(me, k, planes)
        to, slot = route(k)
        return copy_to(to, ask.at[who], asked.at[slot, w], ask_send.at[who], ask_recv.at[slot, w])

    def mate_copy(to, frm):
        return copy_to(
            z * PLANE + to, mate_ask.at[to], mate_asked.at[frm], mate_send.at[to], mate_recv.at[frm]
        )

    def table_copy(way, step, part):
        frm = (z - way * step + planes) % planes
        at = tables.at[frm, pl.ds(part * chunk, chunk)]
        return copy_to(
            (z + way + planes) % planes * PLANE + w,
            at,
            at,
            table_send.at[(way + 1) // 2, step, part],
            table_recv.at[frm, part],
        )

    def row_copy(to, frm, plane):
        return copy_to(
            z * PLANE + to,
            send_rows.at[plane, to],
            got_rows.at[plane * PLANE + frm],
            row_send.at[plane, to],
            row_recv.at[plane * PLANE + frm],
        )

    def grad_copy(k):
        who = partner(me, k, planes)
        to, slot = route(k)
        return copy_to(
            to, send_grads.at[who], got_grads.at[slot, w], grad_send.at[who], grad_recv.at[slot, w]
        )

    parts = side_scale.shape[1]
    part_rows = rows // parts

    def side_copies(side, part):
        at = pl.ds(pl.multiple_of(part * part_rows, part_rows), part_rows)
        to = (z - 1 + 2 * side + planes) % planes * PLANE + w
        return (
            copy_to(
                to,
                side_sum.at[side, at],
                got_sum.at[side, at],
                sum_send.at[side, part],
                sum_recv.at[side, part],
            ),
            copy_to(
                to,
                side_scale.at[side, part],
                got_scale.at[side, part],
                scale_send.at[side, part],
                scale_recv.at[side, part],
            ),
        )

    barrier = pltpu.get_barrier_semaphore()

    def greet(k, carry):
        pl.semaphore_signal(
            barrier,
            inc=1,
            device_id=(bucket, partner(me, k, planes)),
            device_id_type=pl.DeviceIdType.MESH,
        )
        return carry

    lax.fori_loop(1, shards, greet, 0)
    tables[z] = dest_ref[...].astype(BF16)
    pl.semaphore_wait(barrier, shards - 1)

    def halves(late):
        return ((1, int(late)), (-1, 1 - int(late)))

    def pass_on(step, late):
        for way, part in halves(late):
            if step < half - 1 or (step == half - 1 and not late):
                table_copy(way, step, part).start()

    def arrive(step, late):
        for way, part in halves(late):
            if step < half or not late:
                frm = (z - way * step + planes) % planes
                at = tables.at[frm, pl.ds(part * chunk, chunk)]
                copy_to(
                    (z - way + planes) % planes * PLANE + w,
                    at,
                    at,
                    table_send.at[0, 0, 0],
                    table_recv.at[frm, part],
                ).wait_recv()
        pass_on(step, late)

    pass_on(0, False)

    edge_count = count_ref[0].astype(F32)
    edge_owner = edge_owner_ref[...].astype(F32)
    neg_owner = neg_owner_ref[...].astype(F32)
    negs = neg_owner.shape[1]
    edge_hot = ones_where(iota((shards, edges), 0) == edge_owner)
    neg_hot = ones_where(iota((shards, negs), 0) == neg_owner)
    edge_place = running_place(edge_hot)
    neg_place = running_place(neg_hot)
    live_weight[...] = jnp.where(iota((1, edges), 1) < edge_count, neg_weight, 0.0)
    place[...] = jnp.where(iota((1, edges), 1) < edge_count, edge_place, -1.0)

    def asked_ids(hot, rows_ref, slot_row):
        row = rows_ref[...]
        high = (row // 32).astype(F32).astype(BF16)
        low = (row % 32).astype(F32).astype(BF16)
        left = jnp.concatenate([hot * high, hot * low, hot], axis=0)
        at = ones_where(iota((wide, hot.shape[1]), 0) == slot_row)
        return dot(left, at, 1, 1)

    found = asked_ids(edge_hot, edge_rows_ref, edge_place) + asked_ids(
        neg_hot, neg_rows_ref, neg_place + float(edge_slots)
    )
    ids = found[:shards] * 32.0 + found[shards : 2 * shards] + found[2 * shards :] - 1.0
    for owner in range(shards):
        line = ids[owner : owner + 1, :]
        ask[owner] = line
        mate_ask[owner % PLANE, owner // PLANE] = line
    mate_asked[w] = mate_ask[w]
    for k in range(1, PLANE):
        mate_copy((w + k) % PLANE, w).start()

    def start_ask(k, carry):
        ask_copy(k).start()
        return carry

    lax.fori_loop(3 * PLANE, shards, start_ask, 0)
    pass_on(0, True)

    src_hot[...] = ones_where(iota((rows, edges), 0) == src_rows_ref[...].astype(F32))
    source_t = source_ref[...].T.astype(BF16)
    picked_t = dot(source_t, src_hot[...])
    src_t[...] = picked_t.astype(BF16)
    src[...] = picked_t.T.astype(BF16)
    grad_t[...] = jnp.zeros_like(grad_t)
    for k in range(1, PLANE):
        mate_copy((w + k) % PLANE, (w + k) % PLANE).wait_recv()

    def serve(plane):
        hots = []
        for k in range(PLANE):
            line = mate_asked[(w + k) % PLANE, plane]
            spread = jnp.where(iota((slots, wide), 0) == iota((slots, wide), 1), line, 0.0)
            at = jnp.sum(spread, axis=1, keepdims=True)
            hots.append(ones_where(at == iota((slots, rows), 1)))
        found = dot(jnp.concatenate(hots, axis=0), tables[plane]).astype(BF16)
        for k in range(1, PLANE):
            to = (w + k) % PLANE
            send_rows[plane, to] = found[k * slots : (k + 1) * slots]
            row_copy(to, w, plane).start()
        got_rows[plane * PLANE + w] = found[:slots]

    def score(who):
        fetched = got_rows[who]
        targets = fetched[:edge_slots].astype(F32)
        scores = dot(fetched[edge_slots:], src_t[...])
        weight = (live_weight[...] * sigmoid(scores)).astype(BF16)
        weights[who] = weight
        slot_row = jnp.where(edge_owner_ref[...] == who, place[...], -1.0)
        pick = ones_where(iota((edge_slots, edges), 0) == slot_row)
        chosen[who] = pick
        mixed = dot(jnp.concatenate([pick, weight], axis=0), src[...])
        sources = mixed[:edge_slots]
        positive = jnp.sum(sources * targets, axis=1, keepdims=True)
        coef = -sigmoid(-positive)
        part = coef * targets
        high = part.astype(BF16)
        coef_hi[who] = high
        coef_lo[who] = (part - high.astype(F32)).astype(BF16)
        return jnp.concatenate([coef * sources, mixed[edge_slots:]], axis=0).astype(BF16)

    def answer(k, carry):
        who = partner(me, k, planes)
        mine = (w + k) % PLANE

        @pl.when(mine != w)
        def _():
            row_copy(w, mine, who // PLANE).wait_recv()

        grads = score(who)
        to, slot = route(k)

        @pl.when(to == me)
        def _():
            got_grads[slot, w] = grads

        @pl.when(to != me)
        def _():
            send_grads[who] = grads
            grad_copy(k).start()

        return carry

    def serve_next(i, carry):
        serve((z + around(i) + planes) % planes)
        return carry

    serve(z)
    for step in range(1, half + 1):
        arrive(step, False)
        first, last = (2 * step - 3) * PLANE, (2 * step - 1) * PLANE
        if 1 < step < half:
            lax.fori_loop(first, first + PLANE, answer, 0)
            first = first + PLANE
        arrive(step, True)
        lax.fori_loop(2 * step - 1, min(2 * step + 1, planes), serve_next, 0)
        if step == 1:
            got_grads[0, w] = score(me)
        lax.fori_loop(max(first, 1), last, answer, 0)
    lax.fori_loop((planes - 1) * PLANE, shards, answer, 0)

    def source_part(who, carry):
        left = jnp.concatenate([got_rows[who][edge_slots:], coef_hi[who], coef_lo[who]], axis=0)
        right = jnp.concatenate([weights[who], chosen[who], chosen[who]], axis=0)
        grad_t[...] += dot(left, right, 0, 0)
        return carry

    lax.fori_loop(0, shards, source_part, 0)
    source_grad = grad_t[...].T
    high = source_grad.astype(BF16)
    low = (source_grad - high.astype(F32)).astype(BF16)
    new_source_ref[...] = dot(src_hot[...], high) + dot(src_hot[...], low)

    def update_source(i, carry):
        at = pl.ds(pl.multiple_of(i * BLOCK, BLOCK), BLOCK)
        fresh, state = update(new_source_ref[at, :], source_ref, source_state_ref, at)
        new_source_ref[at, :] = fresh
        new_source_state_ref[:, at] = row_of(state)
        return carry

    lax.fori_loop(0, rows // BLOCK, update_source, 0)

    def collect(line, slot, frm):
        hot = ones_where(iota((rows, slots), 0) == line[:, :slots])
        return dot(hot, got_grads[slot, frm])

    def wait_grads(sender, slot, frm):
        at = got_grads.at[slot, frm]
        copy_to(sender, at, at, grad_send.at[0], grad_recv.at[slot, frm]).wait_recv()

    dest_grad[...] = collect(mate_asked[w, z], 0, w)
    side_grad[...] = jnp.zeros_like(side_grad)

    def gather_own(k, carry):
        frm = (w + k) % PLANE
        wait_grads(z * PLANE + frm, 0, frm)
        dest_grad[...] += collect(mate_asked[frm, z], 0, frm)
        return carry

    lax.fori_loop(1, PLANE, gather_own, 0)

    def gather_near(n, carry):
        side, frm = n // PLANE, n % PLANE
        slot = 1 + half * side

        @pl.when(frm != w)
        def _():
            wait_grads(z * PLANE + frm, slot, frm)

        line = mate_asked[frm, (z - 1 + 2 * side + planes) % planes]
        side_grad[side] += collect(line, slot, frm)
        return carry

    lax.fori_loop(0, 2 * PLANE, gather_near, 0)

    def gather_side(size, side, frm):
        slot = size + half * side
        sender = (z + (1 - 2 * side) * (size - 1) + planes) % planes * PLANE + frm
        at = asked.at[slot, frm]
        copy_to(sender, at, at, ask_send.at[0], ask_recv.at[slot, frm]).wait_recv()
        wait_grads(sender, slot, frm)
        side_grad[side] += collect(asked[slot, frm], slot, frm)

    def gather_middle(n, carry):
        gather_side(2 + n // (2 * PLANE), n // PLANE % 2, n % PLANE)
        return carry

    lax.fori_loop(0, (half - 2) * 2 * PLANE, gather_middle, 0)

    def gather_far(n, carry):
        gather_side(half, n // (PLANE // 2), n)
        return carry

    lax.fori_loop(0, PLANE, gather_far, 0)

    def send_sums(part, carry):
        for side in (0, 1):
            for start in range(0, part_rows, BLOCK):
                at = pl.ds(pl.multiple_of(part * part_rows + start, BLOCK), BLOCK)
                total = side_grad[side, at, :]
                largest = jnp.maximum(jnp.max(jnp.abs(total), axis=1, keepdims=True), 1e-30)
                side_sum[side, at, :] = jnp.round(total * (CODE / largest)).astype(jnp.int16)
                side_scale[side, part, :, start : start + BLOCK] = row_of(largest)
            for copy in side_copies(side, part):
                copy.start()
        return carry

    lax.fori_loop(0, parts, send_sums, 0)

    def add_sums(part, carry):
        for side in (0, 1):
            for copy in side_copies(side, part):
                copy.wait_recv()
            for start in range(0, part_rows, BLOCK):
                at = pl.ds(pl.multiple_of(part * part_rows + start, BLOCK), BLOCK)
                scale = column(got_scale[side, part, :, start : start + BLOCK]) * (1.0 / CODE)
                dest_grad[at, :] += got_sum[side, at, :].astype(F32) * scale
        return carry

    lax.fori_loop(0, parts, add_sums, 0)

    def sent(k, carry):
        @pl.when(route(k)[0] != me)
        def _():
            grad_copy(k).wait_send()

        return carry

    lax.fori_loop(1, shards, sent, 0)

    def asks_sent(k, carry):
        ask_copy(k).wait_send()
        return carry

    lax.fori_loop(3 * PLANE, shards, asks_sent, 0)

    def sums_sent(part, carry):
        for side in (0, 1):
            for copy in side_copies(side, part):
                copy.wait_send()
        return carry

    lax.fori_loop(0, parts, sums_sent, 0)
    for k in range(1, PLANE):
        to = (w + k) % PLANE
        mate_copy(to, w).wait_send()

        def rows_sent(plane, carry):
            row_copy(to, w, plane).wait_send()
            return carry

        lax.fori_loop(0, planes, rows_sent, 0)
    for step in range(half):
        for way in (1, -1):
            for part in (0, 1):
                if step < half - 1 or (way, part) in halves(False):
                    table_copy(way, step, part).wait_send()


def device_step(
    dest_slab,
    source_slab,
    source_state,
    source_rows,
    edge_owner,
    edge_rows,
    neg_owner,
    neg_rows,
    edge_count,
):
    shards = lax.axis_size("shard")
    planes = shards // PLANE
    edges = source_rows.shape[0]
    negs = neg_rows.shape[0]
    rows, features = dest_slab.shape
    edge_slots = 3 * edges // (2 * shards)
    neg_slots = 3 * negs // (2 * shards)
    slots = edge_slots + neg_slots
    wide = -(-slots // 128) * 128
    parts = max(1, min(4, rows // BLOCK))
    vmem = pl.BlockSpec(memory_space=pltpu.VMEM)
    dma = pltpu.SemaphoreType.DMA
    return pl.pallas_call(
        functools.partial(step_kernel, edge_slots, negs ** (-0.5)),
        out_shape=(
            jax.ShapeDtypeStruct((rows, features), F32),
            jax.ShapeDtypeStruct((1, rows), F32),
            jax.ShapeDtypeStruct((rows, features), F32),
        ),
        in_specs=[vmem] * 8 + [pl.BlockSpec(memory_space=pltpu.SMEM)],
        out_specs=(vmem,) * 3,
        scratch_shapes=[
            pltpu.VMEM((planes, rows, features), BF16),
            pltpu.VMEM((edges, features), BF16),
            pltpu.VMEM((features, edges), BF16),
            pltpu.VMEM((rows, edges), BF16),
            pltpu.VMEM((1, edges), F32),
            pltpu.VMEM((1, edges), F32),
            pltpu.VMEM((shards, 1, wide), F32),
            pltpu.VMEM((planes + 1, PLANE, 1, wide), F32),
            pltpu.VMEM((PLANE, planes, 1, wide), F32),
            pltpu.VMEM((PLANE, planes, 1, wide), F32),
            pltpu.VMEM((planes, PLANE, slots, features), BF16),
            pltpu.VMEM((shards, slots, features), BF16),
            pltpu.VMEM((shards, slots, features), BF16),
            pltpu.VMEM((planes + 1, PLANE, slots, features), BF16),
            pltpu.VMEM((shards, neg_slots, edges), BF16),
            pltpu.VMEM((shards, edge_slots, edges), BF16),
            pltpu.VMEM((shards, edge_slots, features), BF16),
            pltpu.VMEM((shards, edge_slots, features), BF16),
            pltpu.VMEM((features, edges), F32),
            pltpu.VMEM((2, rows, features), F32),
            pltpu.VMEM((2, rows, features), jnp.int16),
            pltpu.VMEM((2, parts, 1, rows // parts), F32),
            pltpu.VMEM((2, rows, features), jnp.int16),
            pltpu.VMEM((2, parts, 1, rows // parts), F32),
            dma((shards,)),
            dma((planes + 1, PLANE)),
            dma((PLANE,)),
            dma((PLANE,)),
            dma((2, planes // 2, 2)),
            dma((planes, 2)),
            dma((planes, PLANE)),
            dma((shards,)),
            dma((shards,)),
            dma((planes + 1, PLANE)),
            dma((2, parts)),
            dma((2, parts)),
            dma((2, parts)),
            dma((2, parts)),
        ],
        compiler_params=pltpu.CompilerParams(
            collective_id=0, has_side_effects=True, vmem_limit_bytes=58 << 20
        ),
        name="edge_step",
    )(
        dest_slab,
        source_slab,
        source_state[None],
        source_rows[None],
        edge_owner[None],
        edge_rows[None],
        neg_owner[None],
        neg_rows[None],
        edge_count,
    )


def hand_over_kernel(
    mask,
    grad_ref,
    dest_ref,
    state_ref,
    rows_ref,
    new_state_ref,
    coded,
    beside,
    got,
    got_beside,
    send,
    recv,
    beside_send,
    beside_recv,
):
    bucket = lax.axis_index("bucket")
    to = bucket
    for bit in range(mask.bit_length()):
        if mask >> bit & 1:
            to = to + (1 - 2 * (bucket // (1 << bit) % 2)) * (1 << bit)
    to = (to, lax.axis_index("shard"))
    parts = beside.shape[0]
    size = dest_ref.shape[0] // parts

    def copies(part):
        at = pl.ds(part * size, size)
        pairs = (
            (coded.at[at], got.at[at], send, recv),
            (beside.at[part], got_beside.at[part], beside_send, beside_recv),
        )
        return [
            pltpu.make_async_remote_copy(
                src_ref=src_ref,
                dst_ref=dst_ref,
                send_sem=sent.at[part],
                recv_sem=came.at[part],
                device_id=to,
                device_id_type=pl.DeviceIdType.MESH,
            )
            for src_ref, dst_ref, sent, came in pairs
        ]

    barrier = pltpu.get_barrier_semaphore()
    pl.semaphore_signal(barrier, inc=1, device_id=to, device_id_type=pl.DeviceIdType.MESH)
    for part in range(parts):
        for start in range(0, size, BLOCK):
            at = pl.ds(part * size + start, BLOCK)
            fresh, state = update(grad_ref[at, :], dest_ref, state_ref, at)
            largest = jnp.maximum(jnp.max(jnp.abs(fresh), axis=1, keepdims=True), 1e-30)
            coded[at, :] = jnp.round(fresh * (CODE / largest)).astype(jnp.int16)
            beside[part, 0:1, start : start + BLOCK] = row_of(largest)
            beside[part, 1:2, start : start + BLOCK] = row_of(state)
        if part == 0:
            pl.semaphore_wait(barrier, 1)
        for copy in copies(part):
            copy.start()
    for part in range(parts):
        for copy in copies(part):
            copy.wait_recv()
        for start in range(0, size, BLOCK):
            at = pl.ds(part * size + start, BLOCK)
            scale = column(got_beside[part, 0:1, start : start + BLOCK]) * (1.0 / CODE)
            rows_ref[at, :] = got[at, :].astype(F32) * scale
            new_state_ref[:, at] = got_beside[part, 1:2, start : start + BLOCK]
    for part in range(parts):
        for copy in copies(part):
            copy.wait_send()


def hand_over(mask, dest_grad, dest_slab, dest_state):
    rows, features = dest_slab.shape
    parts = max(1, min(4, rows // BLOCK))
    vmem = pl.BlockSpec(memory_space=pltpu.VMEM)
    dma = pltpu.SemaphoreType.DMA
    return pl.pallas_call(
        functools.partial(hand_over_kernel, mask),
        out_shape=(
            jax.ShapeDtypeStruct((rows, features), F32),
            jax.ShapeDtypeStruct((1, rows), F32),
        ),
        in_specs=[vmem] * 3,
        out_specs=(vmem, vmem),
        scratch_shapes=[
            pltpu.VMEM((rows, features), jnp.int16),
            pltpu.VMEM((parts, 2, rows // parts), F32),
            pltpu.VMEM((rows, features), jnp.int16),
            pltpu.VMEM((parts, 2, rows // parts), F32),
            dma((parts,)),
            dma((parts,)),
            dma((parts,)),
            dma((parts,)),
        ],
        compiler_params=pltpu.CompilerParams(
            collective_id=mask, has_side_effects=True, vmem_limit_bytes=32 << 20
        ),
        name="hand_over",
    )(dest_grad, dest_slab, dest_state)


def per_device(
    source_slab,
    source_state,
    dest_slab,
    dest_state,
    source_rows,
    target_owner,
    target_rows,
    negative_owner,
    negative_rows,
    edge_count,
    matching,
):
    new_source, new_source_state, dest_grad = device_step(
        dest_slab,
        source_slab,
        source_state,
        source_rows,
        target_owner[:, 0],
        target_rows,
        negative_owner[:, 0],
        negative_rows,
        edge_count,
    )
    incoming_rows, incoming_state = lax.switch(
        matching[0] - 1,
        [functools.partial(hand_over, mask) for mask in range(1, lax.axis_size("bucket"))],
        dest_grad,
        dest_slab,
        dest_state[None],
    )
    return (new_source, new_source_state[0], incoming_rows, incoming_state[0])


def solution(mesh):
    both = ("bucket", "shard")
    in_specs = (
        P(both, None),
        P(both),
        P(both, None),
        P(both),
        P(both),
        P(both, None),
        P(both),
        P(both, None),
        P(both),
        P(both),
        P(),
    )
    out_specs = (P(both, None), P(both), P(both, None), P(both))
    return jax.shard_map(
        per_device, mesh=mesh, in_specs=in_specs, out_specs=out_specs, check_vma=False
    )
```

```python
import functools

import jax
import jax.numpy as jnp
from jax import lax
from jax.experimental import pallas as pl
from jax.experimental.pallas import tpu as pltpu
from jax.sharding import PartitionSpec as P

learn_rate = 0.1
epsilon = 1e-06
CODE = 32767.0
BLOCK = 128
PLANE = 4
F32, BF16 = jnp.float32, jnp.bfloat16


def sigmoid(x):
    return 0.5 + 0.5 * jnp.tanh(0.5 * x)


def dot(a, b, ca=1, cb=0):
    return lax.dot_general(a, b, (((ca,), (cb,)), ((), ())), preferred_element_type=F32)


def iota(shape, dim):
    return lax.broadcasted_iota(jnp.int32, shape, dim).astype(F32)


def ones_where(mask):
    return jnp.where(mask, 1.0, 0.0).astype(BF16)


def around(i):
    return (i + 1) // 2 * (2 * (i % 2) - 1)


def partner(me, k, planes):
    z = (me // PLANE + around(k // PLANE) + planes) % planes
    return z * PLANE + (me % PLANE + k) % PLANE


def column(row):
    n = row.shape[1]
    return jnp.broadcast_to(row, (n, n)).T[:, :1]


def row_of(col):
    n = col.shape[0]
    return jnp.broadcast_to(col, (n, n)).T[:1, :]


def running_place(onehot):
    owners, n = onehot.shape
    width = 256
    upto = ones_where(iota((width, width), 0) <= iota((width, width), 1))
    carry = jnp.zeros((owners, 1), F32)
    parts = []
    for start in range(0, n, width):
        piece = onehot[:, start : start + width]
        count = dot(piece, upto) + carry
        carry = count[:, width - 1 : width]
        parts.append(jnp.sum(count * piece.astype(F32), axis=0, keepdims=True) - 1.0)
    return jnp.concatenate(parts, axis=1)


def update(grad, table_ref, state_ref, at):
    mean = jnp.sum(grad * grad, axis=1, keepdims=True) * (1.0 / grad.shape[1])
    state = column(state_ref[:, at]) + mean
    return table_ref[at, :] - grad * (learn_rate / (jnp.sqrt(state) + epsilon)), state


def step_kernel(
    edge_slots,
    neg_weight,
    dest_ref,
    source_ref,
    source_state_ref,
    src_rows_ref,
    edge_owner_ref,
    edge_rows_ref,
    neg_owner_ref,
    neg_rows_ref,
    count_ref,
    new_source_ref,
    new_source_state_ref,
    dest_grad,
    tables,
    src,
    src_t,
    src_hot,
    place,
    live_weight,
    ask,
    asked,
    mate_ask,
    mate_asked,
    send_rows,
    got_rows,
    send_grads,
    got_grads,
    weights,
    chosen,
    coef_hi,
    coef_lo,
    grad_t,
    side_grad,
    side_sum,
    side_scale,
    got_sum,
    got_scale,
    ask_send,
    ask_recv,
    mate_send,
    mate_recv,
    table_send,
    table_recv,
    row_send,
    row_recv,
    grad_send,
    grad_recv,
    sum_send,
    sum_recv,
    scale_send,
    scale_recv,
):
    bucket = lax.axis_index("bucket")
    me = lax.axis_index("shard")
    z, w = me // PLANE, me % PLANE
    planes = tables.shape[0]
    half = planes // 2
    shards = planes * PLANE
    edges = src_rows_ref.shape[1]
    rows, features = dest_ref.shape
    chunk = rows // 2
    slots = got_rows.shape[1]
    wide = ask.shape[2]

    def copy_to(to, src_ref, dst_ref, send_sem, recv_sem):
        return pltpu.make_async_remote_copy(
            src_ref=src_ref,
            dst_ref=dst_ref,
            send_sem=send_sem,
            recv_sem=recv_sem,
            device_id=(bucket, to),
            device_id_type=pl.DeviceIdType.MESH,
        )

    def route(k):
        off = around(k // PLANE)
        far = jnp.where(w < PLANE // 2, 1, -1)
        side = jnp.where(off == 0, 0, jnp.where(off < 0, 1, jnp.where(off == half, far, -1)))
        slot = jnp.where(off < 0, -off, off) + jnp.where(side < 0, half, 0)
        plane = (z + off + side + planes) % planes
        return plane * PLANE + (w + k) % PLANE, slot

    def ask_copy(k):
        who = partner(me, k, planes)
        to, slot = route(k)
        return copy_to(to, ask.at[who], asked.at[slot, w], ask_send.at[who], ask_recv.at[slot, w])

    def mate_copy(to, frm):
        return copy_to(
            z * PLANE + to, mate_ask.at[to], mate_asked.at[frm], mate_send.at[to], mate_recv.at[frm]
        )

    def table_copy(way, step, part):
        frm = (z - way * step + planes) % planes
        at = tables.at[frm, pl.ds(part * chunk, chunk)]
        return copy_to(
            (z + way + planes) % planes * PLANE + w,
            at,
            at,
            table_send.at[(way + 1) // 2, step, part],
            table_recv.at[frm, part],
        )

    def row_copy(to, frm, plane):
        return copy_to(
            z * PLANE + to,
            send_rows.at[plane, to],
            got_rows.at[plane * PLANE + frm],
            row_send.at[plane, to],
            row_recv.at[plane * PLANE + frm],
        )

    def grad_copy(k):
        who = partner(me, k, planes)
        to, slot = route(k)
        return copy_to(
            to, send_grads.at[who], got_grads.at[slot, w], grad_send.at[who], grad_recv.at[slot, w]
        )

    parts = side_scale.shape[1]
    part_rows = rows // parts

    def side_copies(side, part):
        at = pl.ds(pl.multiple_of(part * part_rows, part_rows), part_rows)
        to = (z - 1 + 2 * side + planes) % planes * PLANE + w
        return (
            copy_to(
                to,
                side_sum.at[side, at],
                got_sum.at[side, at],
                sum_send.at[side, part],
                sum_recv.at[side, part],
            ),
            copy_to(
                to,
                side_scale.at[side, part],
                got_scale.at[side, part],
                scale_send.at[side, part],
                scale_recv.at[side, part],
            ),
        )

    barrier = pltpu.get_barrier_semaphore()

    def greet(k, carry):
        pl.semaphore_signal(
            barrier,
            inc=1,
            device_id=(bucket, partner(me, k, planes)),
            device_id_type=pl.DeviceIdType.MESH,
        )
        return carry

    lax.fori_loop(1, shards, greet, 0)
    tables[z] = dest_ref[...].astype(BF16)
    pl.semaphore_wait(barrier, shards - 1)

    def halves(late):
        return ((1, int(late)), (-1, 1 - int(late)))

    def pass_on(step, late):
        for way, part in halves(late):
            if step < half - 1 or (step == half - 1 and not late):
                table_copy(way, step, part).start()

    def arrive(step, late):
        for way, part in halves(late):
            if step < half or not late:
                frm = (z - way * step + planes) % planes
                at = tables.at[frm, pl.ds(part * chunk, chunk)]
                copy_to(
                    (z - way + planes) % planes * PLANE + w,
                    at,
                    at,
                    table_send.at[0, 0, 0],
                    table_recv.at[frm, part],
                ).wait_recv()
        pass_on(step, late)

    pass_on(0, False)

    edge_count = count_ref[0].astype(F32)
    edge_owner = edge_owner_ref[...].astype(F32)
    neg_owner = neg_owner_ref[...].astype(F32)
    negs = neg_owner.shape[1]
    edge_hot = ones_where(iota((shards, edges), 0) == edge_owner)
    neg_hot = ones_where(iota((shards, negs), 0) == neg_owner)
    edge_place = running_place(edge_hot)
    neg_place = running_place(neg_hot)
    live_weight[...] = jnp.where(iota((1, edges), 1) < edge_count, neg_weight, 0.0)
    place[...] = jnp.where(iota((1, edges), 1) < edge_count, edge_place, -1.0)

    def asked_ids(hot, rows_ref, slot_row):
        row = rows_ref[...]
        high = (row // 32).astype(F32).astype(BF16)
        low = (row % 32).astype(F32).astype(BF16)
        left = jnp.concatenate([hot * high, hot * low, hot], axis=0)
        at = ones_where(iota((wide, hot.shape[1]), 0) == slot_row)
        return dot(left, at, 1, 1)

    found = asked_ids(edge_hot, edge_rows_ref, edge_place) + asked_ids(
        neg_hot, neg_rows_ref, neg_place + float(edge_slots)
    )
    ids = found[:shards] * 32.0 + found[shards : 2 * shards] + found[2 * shards :] - 1.0
    for owner in range(shards):
        line = ids[owner : owner + 1, :]
        ask[owner] = line
        mate_ask[owner % PLANE, owner // PLANE] = line
    mate_asked[w] = mate_ask[w]
    for k in range(1, PLANE):
        mate_copy((w + k) % PLANE, w).start()

    def start_ask(k, carry):
        ask_copy(k).start()
        return carry

    lax.fori_loop(3 * PLANE, shards, start_ask, 0)
    pass_on(0, True)

    src_hot[...] = ones_where(iota((rows, edges), 0) == src_rows_ref[...].astype(F32))
    source_t = source_ref[...].T.astype(BF16)
    picked_t = dot(source_t, src_hot[...])
    src_t[...] = picked_t.astype(BF16)
    src[...] = picked_t.T.astype(BF16)
    grad_t[...] = jnp.zeros_like(grad_t)
    for k in range(1, PLANE):
        mate_copy((w + k) % PLANE, (w + k) % PLANE).wait_recv()

    def serve(plane):
        hots = []
        for k in range(PLANE):
            line = mate_asked[(w + k) % PLANE, plane]
            spread = jnp.where(iota((slots, wide), 0) == iota((slots, wide), 1), line, 0.0)
            at = jnp.sum(spread, axis=1, keepdims=True)
            hots.append(ones_where(at == iota((slots, rows), 1)))
        found = dot(jnp.concatenate(hots, axis=0), tables[plane]).astype(BF16)
        for k in range(1, PLANE):
            to = (w + k) % PLANE
            send_rows[plane, to] = found[k * slots : (k + 1) * slots]
            row_copy(to, w, plane).start()
        got_rows[plane * PLANE + w] = found[:slots]

    def score(who):
        fetched = got_rows[who]
        targets = fetched[:edge_slots].astype(F32)
        scores = dot(fetched[edge_slots:], src_t[...])
        weight = (live_weight[...] * sigmoid(scores)).astype(BF16)
        weights[who] = weight
        slot_row = jnp.where(edge_owner_ref[...] == who, place[...], -1.0)
        pick = ones_where(iota((edge_slots, edges), 0) == slot_row)
        chosen[who] = pick
        mixed = dot(jnp.concatenate([pick, weight], axis=0), src[...])
        sources = mixed[:edge_slots]
        positive = jnp.sum(sources * targets, axis=1, keepdims=True)
        coef = -sigmoid(-positive)
        part = coef * targets
        high = part.astype(BF16)
        coef_hi[who] = high
        coef_lo[who] = (part - high.astype(F32)).astype(BF16)
        return jnp.concatenate([coef * sources, mixed[edge_slots:]], axis=0).astype(BF16)

    def answer(k, carry):
        who = partner(me, k, planes)
        mine = (w + k) % PLANE

        @pl.when(mine != w)
        def _():
            row_copy(w, mine, who // PLANE).wait_recv()

        grads = score(who)
        to, slot = route(k)

        @pl.when(to == me)
        def _():
            got_grads[slot, w] = grads

        @pl.when(to != me)
        def _():
            send_grads[who] = grads
            grad_copy(k).start()

        return carry

    def serve_next(i, carry):
        serve((z + around(i) + planes) % planes)
        return carry

    serve(z)
    for step in range(1, half + 1):
        arrive(step, False)
        first, last = (2 * step - 3) * PLANE, (2 * step - 1) * PLANE
        if 1 < step < half:
            lax.fori_loop(first, first + PLANE, answer, 0)
            first = first + PLANE
        arrive(step, True)
        lax.fori_loop(2 * step - 1, min(2 * step + 1, planes), serve_next, 0)
        if step == 1:
            got_grads[0, w] = score(me)
        lax.fori_loop(max(first, 1), last, answer, 0)
    lax.fori_loop((planes - 1) * PLANE, shards, answer, 0)

    def collect(line, slot, frm):
        hot = ones_where(iota((rows, slots), 0) == line[:, :slots])
        return dot(hot, got_grads[slot, frm])

    def wait_grads(sender, slot, frm):
        at = got_grads.at[slot, frm]
        copy_to(sender, at, at, grad_send.at[0], grad_recv.at[slot, frm]).wait_recv()

    dest_grad[...] = collect(mate_asked[w, z], 0, w)
    side_grad[...] = jnp.zeros_like(side_grad)

    def gather_own(k, carry):
        frm = (w + k) % PLANE
        wait_grads(z * PLANE + frm, 0, frm)
        dest_grad[...] += collect(mate_asked[frm, z], 0, frm)
        return carry

    lax.fori_loop(1, PLANE, gather_own, 0)

    def gather_near(n, carry):
        side, frm = n // PLANE, n % PLANE
        slot = 1 + half * side

        @pl.when(frm != w)
        def _():
            wait_grads(z * PLANE + frm, slot, frm)

        line = mate_asked[frm, (z - 1 + 2 * side + planes) % planes]
        side_grad[side] += collect(line, slot, frm)
        return carry

    lax.fori_loop(0, 2 * PLANE, gather_near, 0)

    def gather_side(size, side, frm):
        slot = size + half * side
        sender = (z + (1 - 2 * side) * (size - 1) + planes) % planes * PLANE + frm
        at = asked.at[slot, frm]
        copy_to(sender, at, at, ask_send.at[0], ask_recv.at[slot, frm]).wait_recv()
        wait_grads(sender, slot, frm)
        side_grad[side] += collect(asked[slot, frm], slot, frm)

    def gather_middle(n, carry):
        gather_side(2 + n // (2 * PLANE), n // PLANE % 2, n % PLANE)
        return carry

    lax.fori_loop(0, (half - 2) * 2 * PLANE, gather_middle, 0)

    def gather_far(n, carry):
        gather_side(half, n // (PLANE // 2), n)
        return carry

    lax.fori_loop(0, PLANE, gather_far, 0)

    def send_sums(part, carry):
        for side in (0, 1):
            for start in range(0, part_rows, BLOCK):
                at = pl.ds(pl.multiple_of(part * part_rows + start, BLOCK), BLOCK)
                total = side_grad[side, at, :]
                largest = jnp.maximum(jnp.max(jnp.abs(total), axis=1, keepdims=True), 1e-30)
                side_sum[side, at, :] = jnp.round(total * (CODE / largest)).astype(jnp.int16)
                side_scale[side, part, :, start : start + BLOCK] = row_of(largest)
            for copy in side_copies(side, part):
                copy.start()
        return carry

    lax.fori_loop(0, parts, send_sums, 0)

    def source_part(who, carry):
        left = jnp.concatenate([got_rows[who][edge_slots:], coef_hi[who], coef_lo[who]], axis=0)
        right = jnp.concatenate([weights[who], chosen[who], chosen[who]], axis=0)
        grad_t[...] += dot(left, right, 0, 0)
        return carry

    lax.fori_loop(0, shards, source_part, 0)
    source_grad = grad_t[...].T
    high = source_grad.astype(BF16)
    low = (source_grad - high.astype(F32)).astype(BF16)
    new_source_ref[...] = dot(src_hot[...], high) + dot(src_hot[...], low)

    def update_source(i, carry):
        at = pl.ds(pl.multiple_of(i * BLOCK, BLOCK), BLOCK)
        fresh, state = update(new_source_ref[at, :], source_ref, source_state_ref, at)
        new_source_ref[at, :] = fresh
        new_source_state_ref[:, at] = row_of(state)
        return carry

    lax.fori_loop(0, rows // BLOCK, update_source, 0)

    def add_sums(part, carry):
        for side in (0, 1):
            for copy in side_copies(side, part):
                copy.wait_recv()
            for start in range(0, part_rows, BLOCK):
                at = pl.ds(pl.multiple_of(part * part_rows + start, BLOCK), BLOCK)
                scale = column(got_scale[side, part, :, start : start + BLOCK]) * (1.0 / CODE)
                dest_grad[at, :] += got_sum[side, at, :].astype(F32) * scale
        return carry

    lax.fori_loop(0, parts, add_sums, 0)

    def sent(k, carry):
        @pl.when(route(k)[0] != me)
        def _():
            grad_copy(k).wait_send()

        return carry

    lax.fori_loop(1, shards, sent, 0)

    def asks_sent(k, carry):
        ask_copy(k).wait_send()
        return carry

    lax.fori_loop(3 * PLANE, shards, asks_sent, 0)

    def sums_sent(part, carry):
        for side in (0, 1):
            for copy in side_copies(side, part):
                copy.wait_send()
        return carry

    lax.fori_loop(0, parts, sums_sent, 0)
    for k in range(1, PLANE):
        to = (w + k) % PLANE
        mate_copy(to, w).wait_send()

        def rows_sent(plane, carry):
            row_copy(to, w, plane).wait_send()
            return carry

        lax.fori_loop(0, planes, rows_sent, 0)
    for step in range(half):
        for way in (1, -1):
            for part in (0, 1):
                if step < half - 1 or (way, part) in halves(False):
                    table_copy(way, step, part).wait_send()


def device_step(
    dest_slab,
    source_slab,
    source_state,
    source_rows,
    edge_owner,
    edge_rows,
    neg_owner,
    neg_rows,
    edge_count,
):
    shards = lax.axis_size("shard")
    planes = shards // PLANE
    edges = source_rows.shape[0]
    negs = neg_rows.shape[0]
    rows, features = dest_slab.shape
    edge_slots = 3 * edges // (2 * shards)
    neg_slots = 3 * negs // (2 * shards)
    slots = edge_slots + neg_slots
    wide = -(-slots // 128) * 128
    parts = max(1, min(4, rows // BLOCK))
    vmem = pl.BlockSpec(memory_space=pltpu.VMEM)
    dma = pltpu.SemaphoreType.DMA
    return pl.pallas_call(
        functools.partial(step_kernel, edge_slots, negs ** (-0.5)),
        out_shape=(
            jax.ShapeDtypeStruct((rows, features), F32),
            jax.ShapeDtypeStruct((1, rows), F32),
            jax.ShapeDtypeStruct((rows, features), F32),
        ),
        in_specs=[vmem] * 8 + [pl.BlockSpec(memory_space=pltpu.SMEM)],
        out_specs=(vmem,) * 3,
        scratch_shapes=[
            pltpu.VMEM((planes, rows, features), BF16),
            pltpu.VMEM((edges, features), BF16),
            pltpu.VMEM((features, edges), BF16),
            pltpu.VMEM((rows, edges), BF16),
            pltpu.VMEM((1, edges), F32),
            pltpu.VMEM((1, edges), F32),
            pltpu.VMEM((shards, 1, wide), F32),
            pltpu.VMEM((planes + 1, PLANE, 1, wide), F32),
            pltpu.VMEM((PLANE, planes, 1, wide), F32),
            pltpu.VMEM((PLANE, planes, 1, wide), F32),
            pltpu.VMEM((planes, PLANE, slots, features), BF16),
            pltpu.VMEM((shards, slots, features), BF16),
            pltpu.VMEM((shards, slots, features), BF16),
            pltpu.VMEM((planes + 1, PLANE, slots, features), BF16),
            pltpu.VMEM((shards, neg_slots, edges), BF16),
            pltpu.VMEM((shards, edge_slots, edges), BF16),
            pltpu.VMEM((shards, edge_slots, features), BF16),
            pltpu.VMEM((shards, edge_slots, features), BF16),
            pltpu.VMEM((features, edges), F32),
            pltpu.VMEM((2, rows, features), F32),
            pltpu.VMEM((2, rows, features), jnp.int16),
            pltpu.VMEM((2, parts, 1, rows // parts), F32),
            pltpu.VMEM((2, rows, features), jnp.int16),
            pltpu.VMEM((2, parts, 1, rows // parts), F32),
            dma((shards,)),
            dma((planes + 1, PLANE)),
            dma((PLANE,)),
            dma((PLANE,)),
            dma((2, planes // 2, 2)),
            dma((planes, 2)),
            dma((planes, PLANE)),
            dma((shards,)),
            dma((shards,)),
            dma((planes + 1, PLANE)),
            dma((2, parts)),
            dma((2, parts)),
            dma((2, parts)),
            dma((2, parts)),
        ],
        compiler_params=pltpu.CompilerParams(
            collective_id=0, has_side_effects=True, vmem_limit_bytes=58 << 20
        ),
        name="edge_step",
    )(
        dest_slab,
        source_slab,
        source_state[None],
        source_rows[None],
        edge_owner[None],
        edge_rows[None],
        neg_owner[None],
        neg_rows[None],
        edge_count,
    )


def hand_over_kernel(
    mask,
    grad_ref,
    dest_ref,
    state_ref,
    rows_ref,
    new_state_ref,
    coded,
    beside,
    got,
    got_beside,
    send,
    recv,
    beside_send,
    beside_recv,
):
    bucket = lax.axis_index("bucket")
    to = bucket
    for bit in range(mask.bit_length()):
        if mask >> bit & 1:
            to = to + (1 - 2 * (bucket // (1 << bit) % 2)) * (1 << bit)
    to = (to, lax.axis_index("shard"))
    parts, blocks = beside.shape[:2]

    def rows_at(part, block):
        start = (part * blocks + block) * BLOCK
        return pl.ds(pl.multiple_of(start, BLOCK), BLOCK)

    def copies(part):
        size = blocks * BLOCK
        at = pl.ds(pl.multiple_of(part * size, size), size)
        pairs = (
            (coded.at[at], got.at[at], send, recv),
            (beside.at[part], got_beside.at[part], beside_send, beside_recv),
        )
        return [
            pltpu.make_async_remote_copy(
                src_ref=src_ref,
                dst_ref=dst_ref,
                send_sem=sent.at[part],
                recv_sem=came.at[part],
                device_id=to,
                device_id_type=pl.DeviceIdType.MESH,
            )
            for src_ref, dst_ref, sent, came in pairs
        ]

    barrier = pltpu.get_barrier_semaphore()
    pl.semaphore_signal(barrier, inc=1, device_id=to, device_id_type=pl.DeviceIdType.MESH)
    pl.semaphore_wait(barrier, 1)

    def put(part, carry):
        def code(block, carry):
            at = rows_at(part, block)
            fresh, state = update(grad_ref[at, :], dest_ref, state_ref, at)
            largest = jnp.maximum(jnp.max(jnp.abs(fresh), axis=1, keepdims=True), 1e-30)
            coded[at, :] = jnp.round(fresh * (CODE / largest)).astype(jnp.int16)
            beside[part, block, 0:1, :] = row_of(largest)
            beside[part, block, 1:2, :] = row_of(state)
            return carry

        lax.fori_loop(0, blocks, code, 0)
        for copy in copies(part):
            copy.start()
        return carry

    lax.fori_loop(0, parts, put, 0)

    def take(part, carry):
        for copy in copies(part):
            copy.wait_recv()

        def decode(block, carry):
            at = rows_at(part, block)
            scale = column(got_beside[part, block, 0:1, :]) * (1.0 / CODE)
            rows_ref[at, :] = got[at, :].astype(F32) * scale
            new_state_ref[:, at] = got_beside[part, block, 1:2, :]
            return carry

        lax.fori_loop(0, blocks, decode, 0)
        return carry

    lax.fori_loop(0, parts, take, 0)

    def sent(part, carry):
        for copy in copies(part):
            copy.wait_send()
        return carry

    lax.fori_loop(0, parts, sent, 0)


def hand_over(mask, dest_grad, dest_slab, dest_state):
    rows, features = dest_slab.shape
    parts = max(1, min(4, rows // BLOCK))
    vmem = pl.BlockSpec(memory_space=pltpu.VMEM)
    dma = pltpu.SemaphoreType.DMA
    return pl.pallas_call(
        functools.partial(hand_over_kernel, mask),
        out_shape=(
            jax.ShapeDtypeStruct((rows, features), F32),
            jax.ShapeDtypeStruct((1, rows), F32),
        ),
        in_specs=[vmem] * 3,
        out_specs=(vmem, vmem),
        scratch_shapes=[
            pltpu.VMEM((rows, features), jnp.int16),
            pltpu.VMEM((parts, rows // parts // BLOCK, 2, BLOCK), F32),
            pltpu.VMEM((rows, features), jnp.int16),
            pltpu.VMEM((parts, rows // parts // BLOCK, 2, BLOCK), F32),
            dma((parts,)),
            dma((parts,)),
            dma((parts,)),
            dma((parts,)),
        ],
        compiler_params=pltpu.CompilerParams(
            collective_id=mask, has_side_effects=True, vmem_limit_bytes=32 << 20
        ),
        name="hand_over",
    )(dest_grad, dest_slab, dest_state)


def per_device(
    source_slab,
    source_state,
    dest_slab,
    dest_state,
    source_rows,
    target_owner,
    target_rows,
    negative_owner,
    negative_rows,
    edge_count,
    matching,
):
    new_source, new_source_state, dest_grad = device_step(
        dest_slab,
        source_slab,
        source_state,
        source_rows,
        target_owner[:, 0],
        target_rows,
        negative_owner[:, 0],
        negative_rows,
        edge_count,
    )
    incoming_rows, incoming_state = lax.switch(
        matching[0] - 1,
        [functools.partial(hand_over, mask) for mask in range(1, lax.axis_size("bucket"))],
        dest_grad,
        dest_slab,
        dest_state[None],
    )
    return (new_source, new_source_state[0], incoming_rows, incoming_state[0])


def solution(mesh):
    both = ("bucket", "shard")
    in_specs = (
        P(both, None),
        P(both),
        P(both, None),
        P(both),
        P(both),
        P(both, None),
        P(both),
        P(both, None),
        P(both),
        P(both),
        P(),
    )
    out_specs = (P(both, None), P(both), P(both, None), P(both))
    return jax.shard_map(
        per_device, mesh=mesh, in_specs=in_specs, out_specs=out_specs, check_vma=False
    )
```
